32 devices in a mesh: grp: 8 (over z, x), inner: 4 (over y, core).
Axes of the slice: x: 2, y: 2, z: 4, core: 2. Of those that a mesh axis runs over, the one named last changes fastest.
Arguments:
- signal: bfloat16 [64, 1024, 4096], P('grp', None, 'inner'), may hold values from -6 to 6
- bins: int32 [8], replicated, may hold values from 1 to 512, as said below
- mic_positions: float32 [3, 4096], replicated, may hold values from -1 to 1
- grid_positions: float32 [3, 1024], replicated, may hold values from 1 to 3
Outputs:
- beam_map: float32 [8, 1024], replicated
The draws below stay inside these ranges and needn't reach their ends.
Inputs may be any that keep to these rules, and one draw needn't show every extreme that they name: The 8 bins are distinct; bin 1 and bin 1024 / 2 are always among them.
All inputs are finite; a program needn't handle non-finite values.
Results may differ from the reference program's by a relative error of at most 0.02.
Values may be sent and summed in bfloat16 or wider, within the bound.
No kernel may reach another device: no remote copies, remote signals or barrier semaphores. Data moves between devices by JAX's collectives and lax.ppermute only.
A program may use at most 192 MiB of HBM per device.

```python
import math
import jax
import jax.numpy as jnp
from jax import lax

M = 4096
SAMPLES = 1024
F = 8
POINTS = 1024
SNAPS = 64


def draw_bins(key, part):
    inner_key = jax.random.fold_in(key, 11)
    order_key = jax.random.fold_in(key, 23)
    middle = jax.random.permutation(inner_key, SAMPLES // 2 - 2)[:F - 2] + 2
    ends = jnp.array([1, SAMPLES // 2], dtype=jnp.int32)
    chosen = jnp.concatenate([ends, middle.astype(jnp.int32)], 0)
    placing = jax.random.permutation(order_key, F)
    return chosen[placing].astype(jnp.int32)


def levels(own_key, shape, split, smallest, high):
    gain = 1.0
    for axis_at, shards_of in split:
        draws = jax.random.uniform(jax.random.fold_in(jax.random.fold_in(own_key, 6), axis_at), (shards_of,), jnp.float32, smallest / len(split), high / len(split))
        gain = gain * jnp.repeat(jnp.exp(draws), shape[axis_at] // shards_of).reshape((-1,) + (1,) * (len(shape) - 1 - axis_at))
    return gain


def normal_values(stream_key, dims, scale, bound, shards=(), held_as=jnp.bfloat16):
    level = levels(stream_key, dims, shards, -0.22, 0.18) if shards else 1.0
    drawn = jax.random.normal(stream_key, dims, jnp.float32) * scale * level
    return jnp.minimum(jnp.maximum(drawn, -bound), bound).astype(held_as)


def setup_inputs(seed: int = 0) -> dict:
    seeds = jax.random.split(jax.random.key(seed), 5)
    return {
        "signal": normal_values(seeds[0], (SNAPS, SAMPLES, M), 1.0, 6.0, ((0, 8), (2, 4))),
        "bins": draw_bins(jax.random.fold_in(seeds[4], 71), 0),
        "mic_positions": jnp.clip(jax.random.uniform(seeds[2], (3, M), jnp.float32, -1.0, 1.0), -1.0, 1.0),
        "grid_positions": jnp.clip(jax.random.uniform(seeds[3], (3, POINTS), jnp.float32, 1.0, 3.0), 1.0, 3.0),
    }


TWO_PI = 2.0 * math.pi
RATE_OVER_SOUND = 51200.0 / 343.0

def dft_table(bins):
    ticks = jnp.arange(SAMPLES, dtype=jnp.int32)
    turns = bins[:, None] * ticks[None, :] % SAMPLES
    angle = turns.astype(jnp.float32) * (TWO_PI / SAMPLES)
    window = 0.5 - 0.5 * jnp.cos(ticks.astype(jnp.float32) * (TWO_PI / SAMPLES))
    factor = math.sqrt(8.0 / (3.0 * SAMPLES))
    real_part = window[None, :] * jnp.cos(angle) * factor
    imag_part = -window[None, :] * jnp.sin(angle) * factor
    return jnp.concatenate([real_part, imag_part], 0).astype(jnp.bfloat16)

def distances(spots, grid):
    delta_x = grid[0][None, :] - spots[0][:, None]
    delta_y = grid[1][None, :] - spots[1][:, None]
    delta_z = grid[2][None, :] - spots[2][:, None]
    return jnp.sqrt(delta_x * delta_x + delta_y * delta_y + delta_z * delta_z) * RATE_OVER_SOUND

def steering(delay, frequency_bin):
    angle = delay * (frequency_bin.astype(jnp.float32) * (TWO_PI / SAMPLES))
    return jnp.concatenate([jnp.cos(angle), -jnp.sin(angle)], 0).astype(jnp.bfloat16)

def reference(signal, bins, mic_positions, grid_positions):
    table = dft_table(bins)

    def transform(block):
        return jnp.dot(table, block, preferred_element_type=jnp.float32).astype(jnp.bfloat16)
    spectra = lax.map(transform, signal).reshape(SNAPS, 2, F, M)
    delay = distances(mic_positions, grid_positions)
    diagonal_mask = jnp.eye(M, dtype=bool)

    def one_bin(index):
        real_x = spectra[:, 0, index, :]
        imag_x = spectra[:, 1, index, :]
        real_c = jnp.dot(real_x.T, real_x, preferred_element_type=jnp.float32) + jnp.dot(imag_x.T, imag_x, preferred_element_type=jnp.float32)
        imag_c = jnp.dot(imag_x.T, real_x, preferred_element_type=jnp.float32) - jnp.dot(real_x.T, imag_x, preferred_element_type=jnp.float32)
        real_c = jnp.where(diagonal_mask, 0.0, real_c / SNAPS)
        imag_c = jnp.where(diagonal_mask, 0.0, imag_c / SNAPS)
        block = jnp.concatenate([jnp.concatenate([real_c, -imag_c], 1), jnp.concatenate([imag_c, real_c], 1)], 0)
        steer = steering(delay, bins[index]).astype(jnp.float32)
        image = jnp.dot(block, steer, precision=lax.Precision.HIGHEST, preferred_element_type=jnp.float32)
        return lax.optimization_barrier(jnp.sum(steer * image, axis=0))
    partial_value = lax.map(one_bin, jnp.arange(F, dtype=jnp.int32))
    return partial_value * (math.sqrt(SNAPS) / M)
```

```python
import functools
import math

import jax
import jax.numpy as jnp
from jax import lax
from jax.experimental import pallas as pl
from jax.experimental.pallas import tpu as pltpu
from jax.sharding import Mesh, PartitionSpec as P

F = 8
TWO_PI = 2.0 * math.pi
RATE_OVER_SOUND = 51200.0 / 343.0
F32 = jnp.float32
BF16 = jnp.bfloat16
ROUNDER = 12582912.0
LANES = 128

SIN_HALF = (4.4428679027342115, -7.307443409650812, 3.5947879684072226, -0.7843737403612829)
COS_HALF = (1.414204080247352, -6.9776420363098905, 5.715238127798347, -1.7283478206531864)
SIN_FINE = (4.442882937668975, -7.308249445082402, 3.6064748105185624, -0.8474638068718637, 0.11600967661123661, -0.009900200019037797)
COS_FINE = (1.4142135623720369, -6.978864199223495, 5.739885708320473, -1.8883460768140574, 0.33280043358005373, -0.036453250292718266, 0.0026021832760962107)


def polynomial(coefs, u):
    value = coefs[-1] * u + coefs[-2]
    for c in coefs[-3::-1]:
        value = value * u + c
    return value


def cos_sin(turns, sin_half=SIN_HALF, cos_half=COS_HALF):
    r = turns - ((turns + ROUNDER) - ROUNDER)
    u = r * r
    s = polynomial(sin_half, u) * r
    c = polynomial(cos_half, u)
    return 1.0 - s * s, s * c


def dft_table(bins_ref, samples):
    shape = (F, samples)
    row = lax.broadcasted_iota(jnp.int32, shape, 0)
    ticks = lax.broadcasted_iota(jnp.int32, shape, 1)
    bins = jnp.zeros(shape, jnp.int32)
    for f in range(F):
        bins = jnp.where(row == f, bins_ref[f], bins)
    turns = ((bins * ticks) & (samples - 1)).astype(F32) * (1.0 / samples)
    half = ticks.astype(F32) * (1.0 / samples)
    half = half - ((half + ROUNDER) - ROUNDER)
    half_sin = polynomial(SIN_FINE, half * half) * half
    window = 0.5 * half_sin * half_sin * math.sqrt(8.0 / (3.0 * samples))
    cos, sin = cos_sin(turns, SIN_FINE, COS_FINE)
    return jnp.concatenate([window * cos, -window * sin], 0).astype(BF16)


def spread_grid(grid_ref, spread, first):
    for k in range(3):
        for block in range(spread.shape[1] // LANES):
            start = pl.multiple_of(first + block * LANES, LANES)
            line = grid_ref[k : k + 1, pl.ds(start, LANES)]
            spread[k, block * LANES : (block + 1) * LANES, :] = jnp.broadcast_to(line, (LANES, LANES)).T


def steer_rows(row, scale, mic_ref, mic_start, spread, out_row, cos_ref, sin_ref):
    rows = pl.ds(row, 16)
    gx, gy, gz = spread[0, rows, :], spread[1, rows, :], spread[2, rows, :]
    out_rows = pl.ds(out_row, 16)
    at = 0
    for start, width in mic_start:
        for lane in range(0, width, LANES):
            lanes = pl.ds(pl.multiple_of(start + lane, LANES), LANES)
            dx = gx - mic_ref[0:1, lanes]
            dy = gy - mic_ref[1:2, lanes]
            dz = gz - mic_ref[2:3, lanes]
            square = dx * dx + dy * dy + dz * dz
            turns = square * lax.rsqrt(jnp.maximum(square, 1e-30)) * scale
            cos, sin = cos_sin(turns)
            cos_ref[out_rows, at : at + LANES] = cos.astype(BF16)
            sin_ref[out_rows, at : at + LANES] = sin.astype(BF16)
            at += LANES


def mic_order(pairs, width, core):
    return [((2 * pair + lax.rem(core + h, 2)) * width, width) for h in range(2) for pair in range(pairs)]


def turns_per_metre(bins_ref, index, samples):
    return bins_ref[index].astype(F32) * (RATE_OVER_SOUND / samples)


def dft_kernel(pairs, place_ref, bins_ref, mic_ref, grid_ref, signal_ref, out_ref, cos_ref, sin_ref, held, total, spread, sem):
    snaps, samples, mics = held.shape

    def copy(s):
        return pltpu.make_async_copy(signal_ref.at[s], held.at[s], sem.at[s])

    for s in range(snaps):
        copy(s).start()
    index, core = place_ref[0], place_ref[1]
    table = dft_table(bins_ref, samples)
    points = cos_ref.shape[0]
    spread_grid(grid_ref, spread, core * (grid_ref.shape[1] // 2))
    scale = turns_per_metre(bins_ref, index, samples)
    order = mic_order(pairs, mics, core)
    each = points // snaps

    def step(s, carry):
        copy(s).wait()
        total[:, pl.ds(s, 1), :] = jnp.dot(table, held[s], preferred_element_type=F32)[:, None, :]
        for part in range(0, each, 16):
            row = pl.multiple_of(s * each + part, 16)
            steer_rows(row, scale, mic_ref, order, spread, row, cos_ref, sin_ref)
        return carry

    lax.fori_loop(0, snaps, step, 0)
    for f in range(F):
        out_ref[f] = jnp.concatenate([total[f], total[F + f]], 0).astype(BF16)


def steer_kernel(pairs, first, samples, mics, place_ref, bins_ref, mic_ref, grid_ref, cos_ref, sin_ref, spread):
    index, core = place_ref[0], place_ref[1]
    spread_grid(grid_ref, spread, core * (grid_ref.shape[1] // 2) + first)
    scale = turns_per_metre(bins_ref, index, samples)
    order = mic_order(pairs, mics, core)

    def step(i, carry):
        row = pl.multiple_of(i * 16, 16)
        steer_rows(row, scale, mic_ref, order, spread, row, cos_ref, sin_ref)
        return carry

    lax.fori_loop(0, cos_ref.shape[0] // 16, step, 0)


def project_kernel(nears, pairs, own_ref, other_ref, cos_a_ref, sin_a_ref, cos_b_ref, sin_b_ref, out_ref, real_lhs, swap_lhs, power):
    blocks, rows, mics = own_ref.shape
    half = rows // 2
    wide = real_lhs.shape[0]
    real_lhs[...] = jnp.zeros_like(real_lhs)
    swap_lhs[...] = jnp.zeros_like(swap_lhs)
    at = 0
    for ref in (own_ref, other_ref):
        for pair in range(pairs):
            line = jnp.zeros((1, mics), F32)
            for near in range(nears):
                block = ref[near * pairs + pair].astype(F32)
                real_lhs[near * rows : (near + 1) * rows, at : at + mics] = block.astype(BF16)
                swapped = jnp.concatenate([-block[half:], block[:half]], 0)
                swap_lhs[near * rows : (near + 1) * rows, at : at + mics] = swapped.astype(BF16)
                line = line + jnp.sum(block * block, axis=0, keepdims=True)
            power[:, at : at + mics] = jnp.broadcast_to(line, (8, mics))
            at += mics
    point = 0
    chunk = 128
    form = (((1,), (1,)), ((), ()))
    for cos_ref, sin_ref in ((cos_a_ref, sin_a_ref), (cos_b_ref, sin_b_ref)):
        for start in range(0, cos_ref.shape[0], chunk):
            cos = cos_ref[start : start + chunk, :]
            sin = sin_ref[start : start + chunk, :]
            y = lax.dot_general(cos, real_lhs[...], form, preferred_element_type=F32)
            y = y + lax.dot_general(sin, swap_lhs[...], form, preferred_element_type=F32)
            lane_sums = []
            for row in range(0, chunk, 16):
                acc = jnp.zeros((16, LANES), F32)
                for lane in range(0, at, LANES):
                    c = cos_ref[start + row : start + row + 16, lane : lane + LANES].astype(F32)
                    d = sin_ref[start + row : start + row + 16, lane : lane + LANES].astype(F32)
                    acc = acc + (c * c + d * d) * power[0:1, lane : lane + LANES]
                lane_sums.append(acc)
            diagonal = jnp.concatenate(lane_sums, 0)
            value = y * y
            part = value[:, :LANES]
            for lane in range(LANES, wide, LANES):
                part = part + value[:, lane : lane + LANES]
            line = jnp.sum((part - diagonal).T, axis=0, keepdims=True)
            out_ref[:, point // LANES : point // LANES + 1, :] = jnp.broadcast_to(line[None], (out_ref.shape[0], 1, LANES))
            point += chunk


def shards(nears, pairs, devices, signal, bins, mic_positions, grid_positions):
    snaps, samples, mics = signal.shape
    total_mics = mic_positions.shape[1]
    points = grid_positions.shape[1]
    half_points = points // 2
    shadow = half_points // 2
    rest = half_points - shadow
    core = lax.axis_index("core")
    place = jnp.stack([lax.axis_index("near") * pairs + lax.axis_index("pair"), core]).astype(jnp.int32)
    vmem = pl.BlockSpec(memory_space=pltpu.VMEM)
    smem = pl.BlockSpec(memory_space=pltpu.SMEM)
    params = pltpu.CompilerParams(vmem_limit_bytes=40 * 2**20)
    steer_cost = pl.CostEstimate(flops=40 * rest * total_mics, bytes_accessed=4 * rest * total_mics, transcendentals=rest * total_mics)
    steer_shape = [jax.ShapeDtypeStruct((shadow, total_mics), BF16)] * 2
    local, cos_a, sin_a = pl.pallas_call(
        functools.partial(dft_kernel, pairs),
        in_specs=[smem, smem, vmem, vmem, pl.BlockSpec(memory_space=pl.ANY)],
        out_specs=[vmem] * 3,
        out_shape=[jax.ShapeDtypeStruct((F, 2 * snaps, mics), BF16)] + steer_shape,
        scratch_shapes=[
            pltpu.VMEM((snaps, samples, mics), BF16),
            pltpu.VMEM((2 * F, snaps, mics), F32),
            pltpu.VMEM((3, shadow, LANES), F32),
            pltpu.SemaphoreType.DMA((snaps,)),
        ],
        compiler_params=params,
        name="dft_and_steering",
    )(place, bins, mic_positions, grid_positions, signal)
    own = lax.all_to_all(local, ("near", "pair"), 0, 0, tiled=True)
    cos_b, sin_b = pl.pallas_call(
        functools.partial(steer_kernel, pairs, shadow, samples, mics),
        in_specs=[smem, smem, vmem, vmem],
        out_specs=[vmem] * 2,
        out_shape=[jax.ShapeDtypeStruct((rest, total_mics), BF16)] * 2,
        scratch_shapes=[pltpu.VMEM((3, rest, LANES), F32)],
        compiler_params=pltpu.CompilerParams(vmem_limit_bytes=16 * 2**20),
        cost_estimate=steer_cost,
        name="steering",
    )(place, bins, mic_positions, grid_positions)
    other = lax.ppermute(own, "core", [(0, 1), (1, 0)])
    rows = nears * 2 * snaps
    wide = -(-rows // LANES) * LANES
    mine = pl.pallas_call(
        functools.partial(project_kernel, nears, pairs),
        in_specs=[vmem] * 6,
        out_specs=vmem,
        out_shape=jax.ShapeDtypeStruct((devices, half_points // LANES, LANES), F32),
        scratch_shapes=[
            pltpu.VMEM((wide, total_mics), BF16),
            pltpu.VMEM((wide, total_mics), BF16),
            pltpu.VMEM((8, total_mics), F32),
        ],
        compiler_params=pltpu.CompilerParams(vmem_limit_bytes=24 * 2**20),
        name="projection",
    )(own, other, cos_a, sin_a, cos_b, sin_b)
    axes = ("wide", "near", "pair", "core")
    everyone = lax.all_to_all(mine, axes, 0, 0, tiled=True)
    summed = jnp.sum(everyone.reshape(-1, F, points), axis=0)
    all_snaps = snaps * lax.axis_size("wide") * nears
    return summed * (1.0 / (math.sqrt(all_snaps) * total_mics))


def solution(mesh):
    groups, inner = mesh.shape["grp"], mesh.shape["inner"]
    pairs = inner // 2
    nears = F // pairs
    fine = Mesh(mesh.devices.reshape(groups // nears, nears, pairs, 2), ("wide", "near", "pair", "core"))
    in_specs = (P(("wide", "near"), None, ("pair", "core")), P(), P(), P())
    step = functools.partial(shards, nears, pairs, groups * inner)
    return jax.shard_map(step, mesh=fine, in_specs=in_specs, out_specs=P(), check_vma=False)
```

```python
import functools
import math

import jax
import jax.numpy as jnp
from jax import lax
from jax.experimental import pallas as pl
from jax.experimental.pallas import tpu as pltpu
from jax.sharding import Mesh, PartitionSpec as P

F = 8
TWO_PI = 2.0 * math.pi
RATE_OVER_SOUND = 51200.0 / 343.0
F32 = jnp.float32
BF16 = jnp.bfloat16
ROUNDER = 12582912.0
LANES = 128
DEPTH = 64
STEP = 512
COLUMNS = 256

SIN_HALF = (4.4428679027342115, -7.307443409650812, 3.5947879684072226, -0.7843737403612829)
COS_HALF = (1.414204080247352, -6.9776420363098905, 5.715238127798347, -1.7283478206531864)
SIN_FINE = (4.442882937668975, -7.308249445082402, 3.6064748105185624, -0.8474638068718637, 0.11600967661123661, -0.009900200019037797)
COS_FINE = (1.4142135623720369, -6.978864199223495, 5.739885708320473, -1.8883460768140574, 0.33280043358005373, -0.036453250292718266, 0.0026021832760962107)


def polynomial(coefs, u):
    value = coefs[-1] * u + coefs[-2]
    for c in coefs[-3::-1]:
        value = value * u + c
    return value


def cos_sin(turns, sin_half=SIN_HALF, cos_half=COS_HALF):
    r = turns - ((turns + ROUNDER) - ROUNDER)
    u = r * r
    s = polynomial(sin_half, u) * r
    c = polynomial(cos_half, u)
    return 1.0 - s * s, s * c


def dft_table(bins_ref, samples):
    shape = (F, samples)
    row = lax.broadcasted_iota(jnp.int32, shape, 0)
    ticks = lax.broadcasted_iota(jnp.int32, shape, 1)
    bins = jnp.zeros(shape, jnp.int32)
    for f in range(F):
        bins = jnp.where(row == f, bins_ref[f], bins)
    turns = ((bins * ticks) & (samples - 1)).astype(F32) * (1.0 / samples)
    half = ticks.astype(F32) * (1.0 / samples)
    half = half - ((half + ROUNDER) - ROUNDER)
    half_sin = polynomial(SIN_FINE, half * half) * half
    window = 0.5 * half_sin * half_sin * math.sqrt(8.0 / (3.0 * samples))
    cos, sin = cos_sin(turns, SIN_FINE, COS_FINE)
    return jnp.concatenate([window * cos, -window * sin], 0).astype(BF16)


def split(value):
    high = value.astype(BF16).astype(F32)
    rest = value - high
    middle = rest.astype(BF16).astype(F32)
    return high, middle, rest - middle


def pairs_of(groups):
    return [jnp.concatenate([groups[i], groups[i + 1]], 0) for i in range(0, len(groups), 2)]


def distance_factors(scale, mic_ref, order, grid_ref, grid_start, rows8, left_ref, right_ref):
    at = 0
    for start, width in order:
        near = (1.0 - mic_ref[:, pl.ds(pl.multiple_of(start, LANES), width)]) * scale
        rows8[0:3, at : at + width] = near + near
        rows8[3:4, at : at + width] = jnp.sum(near * near, axis=0, keepdims=True)
        at += width
    rows8[4:5, :] = jnp.ones((1, at), F32)
    rows8[5:8, :] = jnp.zeros((3, at), F32)
    high, middle, low = split(rows8[...])
    for i, rows in enumerate(pairs_of([high, middle, low, high, middle, low, high, middle])):
        right_ref[16 * i : 16 * i + 16, :] = rows.astype(BF16)
    points = left_ref.shape[0]
    far = (grid_ref[:, pl.ds(pl.multiple_of(grid_start, LANES), points)] - 1.0) * scale
    rows8[0:3, :points] = far
    rows8[3:4, :points] = jnp.ones((1, points), F32)
    rows8[4:5, :points] = jnp.sum(far * far, axis=0, keepdims=True) + 1e-30
    high, middle, low = split(rows8[:, :points])
    groups = [high, high, high, middle, middle, middle, low, low]
    zeros = jnp.zeros((LANES - DEPTH, points), F32)
    left_ref[...] = jnp.concatenate(groups + [zeros], 0).T.astype(BF16)


def steer_rows(row, out_row, count, lanes, left_ref, right_ref, cos_ref, sin_ref):
    left = left_ref[pl.ds(row, count), 0:DEPTH]
    out_rows = pl.ds(out_row, count)
    step = lanes.step
    for at in lanes:
        square = jnp.dot(left, right_ref[0:DEPTH, at : at + step], preferred_element_type=F32)
        cos, sin = cos_sin(square * lax.rsqrt(square))
        cos_ref[out_rows, at : at + step] = cos.astype(BF16)
        sin_ref[out_rows, at : at + step] = sin.astype(BF16)


def mic_order(pairs, width, core):
    return [((2 * pair + lax.rem(core + h, 2)) * width, width) for h in range(2) for pair in range(pairs)]


def dft_kernel(
    pairs, place_ref, bins_hbm, mic_hbm, grid_hbm, signal_ref,
    out_ref, cos_ref, sin_ref, left_ref, right_ref,
    held, total, bins_ref, mic_ref, grid_ref, rows8, small_sem, sem,
):
    snaps, samples, mics = held.shape
    small = [
        pltpu.make_async_copy(source, target, small_sem.at[i])
        for i, (source, target) in enumerate([(bins_hbm, bins_ref), (mic_hbm, mic_ref), (grid_hbm, grid_ref)])
    ]

    def copy(s):
        return pltpu.make_async_copy(signal_ref.at[s], held.at[s], sem.at[s])

    for c in small:
        c.start()
    for s in range(snaps):
        copy(s).start(priority=1)
    for c in small:
        c.wait()
    index, core = place_ref[0], place_ref[1]
    scale = bins_ref[index].astype(F32) * (RATE_OVER_SOUND / samples)
    order = mic_order(pairs, mics, core)
    distance_factors(scale, mic_ref, order, grid_ref, core * (grid_ref.shape[1] // 2), rows8, left_ref, right_ref)
    table = dft_table(bins_ref, samples)
    each = cos_ref.shape[0] // snaps
    parts = max(mics // COLUMNS, 1)
    columns = mics // parts
    width = right_ref.shape[1] // parts

    def steer(s, part):
        row = pl.multiple_of(s * each, 16)
        lanes = range(part * width, (part + 1) * width, min(STEP, width))
        steer_rows(row, row, each, lanes, left_ref, right_ref, cos_ref, sin_ref)

    def transform(s, part):
        across = slice(part * columns, (part + 1) * columns)
        total[:, pl.ds(s, 1), across] = jnp.dot(table, held[s, :, across], preferred_element_type=F32)[:, None, :]

    def step(s, carry):
        copy(s).wait()
        for part in range(parts):
            transform(s, part)
            steer(s + 1, part)
        return carry

    for part in range(parts):
        steer(0, part)
    lax.fori_loop(0, snaps - 1, step, 0)
    copy(snaps - 1).wait()
    for part in range(parts):
        transform(snaps - 1, part)
    for f in range(F):
        out_ref[f] = jnp.concatenate([total[f], total[F + f]], 0).astype(BF16)


def project(nears, pairs, side, x_ref, cos_ref, sin_ref, real_lhs, swap_lhs, power, use):
    blocks, rows, mics = x_ref.shape
    half = rows // 2
    used = nears * rows
    if used < real_lhs.shape[0]:
        real_lhs[used:, :] = jnp.zeros((real_lhs.shape[0] - used, real_lhs.shape[1]), BF16)
        swap_lhs[used:, :] = jnp.zeros((real_lhs.shape[0] - used, real_lhs.shape[1]), BF16)
    for pair in range(pairs):
        lanes = slice(pair * mics, (pair + 1) * mics)
        squares = jnp.zeros((half, mics), F32)
        for near in range(nears):
            block = x_ref[near * pairs + pair]
            real_lhs[near * rows : (near + 1) * rows, lanes] = block
            block = block.astype(F32)
            top, low = block[:half], block[half:]
            swap_lhs[near * rows : (near + 1) * rows, lanes] = jnp.concatenate([-low, top], 0).astype(BF16)
            squares = squares + (top * top + low * low)
        power[:, lanes] = jnp.broadcast_to(jnp.sum(squares, axis=0, keepdims=True), (8, mics))
    width = pairs * mics
    first = side * width
    form = (((1,), (1,)), ((), ()))
    step = min(STEP, width)
    for point in range(0, cos_ref.shape[0], LANES):
        rows_now = slice(point, point + LANES)
        y = jnp.zeros((LANES, real_lhs.shape[0]), F32)
        sums = [jnp.zeros((16, LANES), F32)] * (LANES // 16)
        for at in range(0, width, step):
            across = slice(first + at, first + at + step)
            y = y + lax.dot_general(cos_ref[rows_now, across], real_lhs[:, at : at + step], form, preferred_element_type=F32)
            y = y + lax.dot_general(sin_ref[rows_now, across], swap_lhs[:, at : at + step], form, preferred_element_type=F32)
            for lane in range(at, at + step, LANES):
                weight = power[0:1, lane : lane + LANES]
                lanes = slice(first + lane, first + lane + LANES)
                for i in range(LANES // 16):
                    c = cos_ref[point + 16 * i : point + 16 * i + 16, lanes].astype(F32)
                    d = sin_ref[point + 16 * i : point + 16 * i + 16, lanes].astype(F32)
                    sums[i] = sums[i] + (c * c + d * d) * weight
        use(point, y, jnp.concatenate(sums, 0))


def own_kernel(nears, pairs, x_ref, cos_ref, sin_ref, y_ref, diagonal_ref, real_lhs, swap_lhs, power):
    def use(point, y, diagonal):
        y_ref[point : point + LANES, :] = y
        diagonal_ref[point : point + LANES, :] = diagonal

    project(nears, pairs, 0, x_ref, cos_ref, sin_ref, real_lhs, swap_lhs, power, use)


def other_kernel(
    nears, pairs, x_ref, cos_ref, sin_ref, y_ref, diagonal_ref, out_ref, real_lhs, swap_lhs, power
):
    def use(point, y, diagonal):
        y = y + y_ref[point : point + LANES, :]
        value = y * y
        part = value[:, :LANES]
        for lane in range(LANES, value.shape[1], LANES):
            part = part + value[:, lane : lane + LANES]
        part = part - (diagonal + diagonal_ref[point : point + LANES, :])
        line = jnp.sum(part.T, axis=0, keepdims=True)
        at = point // LANES
        out_ref[:, at : at + 1, :] = jnp.broadcast_to(line[None], (out_ref.shape[0], 1, LANES))

    project(nears, pairs, 1, x_ref, cos_ref, sin_ref, real_lhs, swap_lhs, power, use)


def shards(nears, pairs, devices, signal, bins, mic_positions, grid_positions):
    snaps, samples, mics = signal.shape
    total_mics = mic_positions.shape[1]
    points = grid_positions.shape[1]
    half_points = points // 2
    place = jnp.stack([lax.axis_index("near") * pairs + lax.axis_index("pair"), lax.axis_index("core")]).astype(jnp.int32)
    vmem = pl.BlockSpec(memory_space=pltpu.VMEM)
    smem = pl.BlockSpec(memory_space=pltpu.SMEM)
    anywhere = pl.BlockSpec(memory_space=pl.ANY)

    def steer_shape(count):
        return [pltpu.VMEM((count, total_mics), BF16)] * 2

    def in_hbm(array):
        return pltpu.with_memory_space_constraint(array, pltpu.HBM)

    def in_vmem(array):
        return pltpu.with_memory_space_constraint(array, pltpu.VMEM)

    local, cos, sin = pl.pallas_call(
        functools.partial(dft_kernel, pairs),
        in_specs=[smem, anywhere, anywhere, anywhere, anywhere],
        out_specs=[vmem] * 3,
        out_shape=[
            jax.ShapeDtypeStruct((F, 2 * snaps, mics), BF16),
            *steer_shape(half_points),
        ],
        scratch_shapes=[
            pltpu.VMEM((half_points, LANES), BF16),
            pltpu.VMEM((DEPTH, total_mics), BF16),
            pltpu.VMEM((snaps, samples, mics), BF16),
            pltpu.VMEM((2 * F, snaps, mics), F32),
            pltpu.SMEM(bins.shape, jnp.int32),
            pltpu.VMEM(mic_positions.shape, F32),
            pltpu.VMEM(grid_positions.shape, F32),
            pltpu.VMEM((8, total_mics), F32),
            pltpu.SemaphoreType.DMA((3,)),
            pltpu.SemaphoreType.DMA((snaps,)),
        ],
        compiler_params=pltpu.CompilerParams(vmem_limit_bytes=24 * 2**20),
        name="dft_and_steering",
    )(place, in_hbm(bins), in_hbm(mic_positions), in_hbm(grid_positions), in_hbm(signal))
    own = lax.all_to_all(local, ("near", "pair"), 0, 0, tiled=True)
    other = lax.ppermute(own, "core", [(0, 1), (1, 0)])
    wide = -(-nears * 2 * snaps // LANES) * LANES
    side_mics = total_mics // 2
    scratch = [
        pltpu.VMEM((wide, side_mics), BF16),
        pltpu.VMEM((wide, side_mics), BF16),
        pltpu.VMEM((8, side_mics), F32),
    ]
    steer = (in_vmem(cos), in_vmem(sin))
    cost = pl.CostEstimate(
        flops=4 * half_points * wide * side_mics, bytes_accessed=4 * half_points * side_mics, transcendentals=0
    )
    y, diagonal = pl.pallas_call(
        functools.partial(own_kernel, nears, pairs),
        in_specs=[vmem] * 3,
        out_specs=[vmem] * 2,
        out_shape=[pltpu.VMEM((half_points, wide), F32), pltpu.VMEM((half_points, LANES), F32)],
        scratch_shapes=scratch,
        compiler_params=pltpu.CompilerParams(vmem_limit_bytes=8 * 2**20),
        cost_estimate=cost,
        name="own_projection",
    )(own, *steer)
    mine = pl.pallas_call(
        functools.partial(other_kernel, nears, pairs),
        in_specs=[vmem] * 5,
        out_specs=vmem,
        out_shape=jax.ShapeDtypeStruct((devices, half_points // LANES, LANES), F32),
        scratch_shapes=scratch,
        compiler_params=pltpu.CompilerParams(vmem_limit_bytes=8 * 2**20),
        cost_estimate=cost,
        name="other_projection",
    )(other, *steer, in_vmem(y), in_vmem(diagonal))
    axes = ("wide", "near", "pair", "core")
    everyone = lax.all_to_all(mine, axes, 0, 0, tiled=True)
    summed = jnp.sum(everyone.reshape(-1, F, points), axis=0)
    all_snaps = snaps * lax.axis_size("wide") * nears
    return summed * (1.0 / (math.sqrt(all_snaps) * total_mics))


def solution(mesh):
    groups, inner = mesh.shape["grp"], mesh.shape["inner"]
    pairs = inner // 2
    nears = F // pairs
    fine = Mesh(mesh.devices.reshape(groups // nears, nears, pairs, 2), ("wide", "near", "pair", "core"))
    in_specs = (P(("wide", "near"), None, ("pair", "core")), P(), P(), P())
    step = functools.partial(shards, nears, pairs, groups * inner)
    return jax.shard_map(step, mesh=fine, in_specs=in_specs, out_specs=P(), check_vma=False)
```

```python
import functools
import math

import jax
import jax.numpy as jnp
from jax import lax
from jax.experimental import pallas as pl
from jax.experimental.pallas import tpu as pltpu
from jax.sharding import Mesh, PartitionSpec as P

F = 8
TWO_PI = 2.0 * math.pi
RATE_OVER_SOUND = 51200.0 / 343.0
F32 = jnp.float32
BF16 = jnp.bfloat16
ROUNDER = 12582912.0
LANES = 128
DEPTH = 64
STEP = 512
COLUMNS = 256

SIN_HALF = (4.441535724093539, -7.264680926673255, 3.25204996020452)
COS_HALF = (1.414204080247352, -6.9776420363098905, 5.715238127798347, -1.7283478206531864)
SIN_FINE = (4.442882937668975, -7.308249445082402, 3.6064748105185624, -0.8474638068718637, 0.11600967661123661, -0.009900200019037797)
COS_FINE = (1.4142135623720369, -6.978864199223495, 5.739885708320473, -1.8883460768140574, 0.33280043358005373, -0.036453250292718266, 0.0026021832760962107)


def polynomial(coefs, u):
    value = coefs[-1] * u + coefs[-2]
    for c in coefs[-3::-1]:
        value = value * u + c
    return value


def cos_sin(turns, sin_half=SIN_HALF, cos_half=COS_HALF):
    r = turns - ((turns + ROUNDER) - ROUNDER)
    u = r * r
    s = polynomial(sin_half, u) * r
    c = polynomial(cos_half, u)
    return c * c - 1.0, s * c


def dft_table(bins_ref, samples):
    shape = (F, samples)
    row = lax.broadcasted_iota(jnp.int32, shape, 0)
    ticks = lax.broadcasted_iota(jnp.int32, shape, 1)
    bins = jnp.zeros(shape, jnp.int32)
    for f in range(F):
        bins = jnp.where(row == f, bins_ref[f], bins)
    turns = ((bins * ticks) & (samples - 1)).astype(F32) * (1.0 / samples)
    half = ticks.astype(F32) * (1.0 / samples)
    half = half - ((half + ROUNDER) - ROUNDER)
    half_sin = polynomial(SIN_FINE, half * half) * half
    window = 0.5 * half_sin * half_sin * math.sqrt(8.0 / (3.0 * samples))
    cos, sin = cos_sin(turns, SIN_FINE, COS_FINE)
    return jnp.concatenate([window * cos, -window * sin], 0).astype(BF16)


def split(value):
    high = value.astype(BF16).astype(F32)
    rest = value - high
    middle = rest.astype(BF16).astype(F32)
    return high, middle, rest - middle


def pairs_of(groups):
    return [jnp.concatenate([groups[i], groups[i + 1]], 0) for i in range(0, len(groups), 2)]


def distance_factors(scale, mic_ref, order, grid_ref, grid_start, rows8, left_ref, right_ref):
    at = 0
    for start, width in order:
        near = (1.0 - mic_ref[:, pl.ds(pl.multiple_of(start, LANES), width)]) * scale
        rows8[0:3, at : at + width] = near + near
        rows8[3:4, at : at + width] = jnp.sum(near * near, axis=0, keepdims=True)
        at += width
    rows8[4:5, :] = jnp.ones((1, at), F32)
    rows8[5:8, :] = jnp.zeros((3, at), F32)
    high, middle, low = split(rows8[...])
    for i, rows in enumerate(pairs_of([high, middle, low, high, middle, low, high, middle])):
        right_ref[16 * i : 16 * i + 16, :] = rows.astype(BF16)
    points = left_ref.shape[0]
    far = (grid_ref[:, pl.ds(pl.multiple_of(grid_start, LANES), points)] - 1.0) * scale
    rows8[0:3, :points] = far
    rows8[3:4, :points] = jnp.ones((1, points), F32)
    rows8[4:5, :points] = jnp.sum(far * far, axis=0, keepdims=True) + 1e-30
    high, middle, low = split(rows8[:, :points])
    groups = [high, high, high, middle, middle, middle, low, low]
    zeros = jnp.zeros((LANES - DEPTH, points), F32)
    left_ref[...] = jnp.concatenate(groups + [zeros], 0).T.astype(BF16)


def steer_block(row, row_end, at, width, left_ref, right_ref, cos_ref, sin_ref):
    lanes = slice(at, at + width)
    square = jnp.dot(left_ref[row:row_end, 0:DEPTH], right_ref[0:DEPTH, lanes], preferred_element_type=F32)
    cos, sin = cos_sin(square * lax.rsqrt(square))
    cos_ref[row:row_end, lanes] = cos.astype(BF16)
    sin_ref[row:row_end, lanes] = sin.astype(BF16)


def stages(snaps, points):
    first = max(points * 5 // 16 // 16 * 16, 16)
    second = first + (points - first) // 32 * 16
    return [(0, first), (snaps // 2, second), (snaps, points)]


def interleaved(left, right):
    count = max(len(left), len(right))
    for i in range(count):
        yield tuple(work[i * len(work) // count : (i + 1) * len(work) // count] for work in (left, right))


def mic_order(pairs, width, core):
    return [((2 * pair + lax.rem(core + h, 2)) * width, width) for h in range(2) for pair in range(pairs)]


def dft_kernel(
    pairs, place_ref, bins_hbm, mic_hbm, grid_hbm, signal_ref,
    out_ref, cos_ref, sin_ref, left_ref, right_ref,
    held, total, bins_ref, mic_ref, grid_ref, rows8, small_sem, sem,
):
    snaps, samples, mics = held.shape
    small = [
        pltpu.make_async_copy(source, target, small_sem.at[i])
        for i, (source, target) in enumerate([(bins_hbm, bins_ref), (mic_hbm, mic_ref), (grid_hbm, grid_ref)])
    ]

    def copy(s):
        return pltpu.make_async_copy(signal_ref.at[s], held.at[s], sem.at[s])

    for c in small:
        c.start()
    for s in range(snaps):
        copy(s).start(priority=1)
    for c in small:
        c.wait()
    index, core = place_ref[0], place_ref[1]
    scale = bins_ref[index].astype(F32) * (RATE_OVER_SOUND / samples)
    order = mic_order(pairs, mics, core)
    distance_factors(scale, mic_ref, order, grid_ref, core * (grid_ref.shape[1] // 2), rows8, left_ref, right_ref)
    table = dft_table(bins_ref, samples)

    def transform(s, at, width):
        across = slice(at, at + width)
        total[:, s : s + 1, across] = jnp.dot(table, held[s, :, across], preferred_element_type=F32)[:, None, :]

    columns = min(COLUMNS, mics)
    points, lanes = cos_ref.shape
    step = min(STEP, lanes)
    row = snap = 0
    for snap_end, row_end in stages(snaps, points):
        for s in range(snap, snap_end):
            copy(s).wait()
        transforms = [(s, at, columns) for s in range(snap, snap_end) for at in range(0, mics, columns)]
        steerings = [(row, row_end, at, step) for at in range(0, lanes, step)]
        for take_transforms, take_steerings in interleaved(transforms, steerings):
            for args in take_transforms:
                transform(*args)
            for args in take_steerings:
                steer_block(*args, left_ref, right_ref, cos_ref, sin_ref)
        row, snap = row_end, snap_end
    for f in range(F):
        out_ref[f] = jnp.concatenate([total[f], total[F + f]], 0).astype(BF16)


def project(nears, pairs, side, x_ref, cos_ref, sin_ref, real_lhs, swap_lhs, power):
    blocks, rows, mics = x_ref.shape
    half = rows // 2
    for pair in range(pairs):
        lanes = slice(pair * mics, (pair + 1) * mics)
        squares = jnp.zeros((half, mics), F32)
        for near in range(nears):
            block = x_ref[near * pairs + pair]
            real_lhs[near * rows : (near + 1) * rows, lanes] = block
            block = block.astype(F32)
            top, low = block[:half], block[half:]
            swap_lhs[near * rows : (near + 1) * rows, lanes] = jnp.concatenate([-low, top], 0).astype(BF16)
            squares = squares + (top * top + low * low)
        power[:, lanes] = jnp.broadcast_to(jnp.sum(squares, axis=0, keepdims=True), (8, mics))
    width = pairs * mics
    first = side * width
    form = (((1,), (1,)), ((), ()))
    step = min(STEP, width)
    points = cos_ref.shape[0]
    y = jnp.zeros((points, real_lhs.shape[0]), F32)
    sums = [jnp.zeros((16, LANES), F32)] * (points // 16)
    for at in range(0, width, step):
        across = slice(first + at, first + at + step)
        y = y + lax.dot_general(cos_ref[:, across], real_lhs[:, at : at + step], form, preferred_element_type=F32)
        y = y + lax.dot_general(sin_ref[:, across], swap_lhs[:, at : at + step], form, preferred_element_type=F32)
        for i in range(points // 16):
            for lane in range(at, at + step, LANES):
                weight = power[0:1, lane : lane + LANES]
                lanes = slice(first + lane, first + lane + LANES)
                c = cos_ref[16 * i : 16 * i + 16, lanes].astype(F32)
                d = sin_ref[16 * i : 16 * i + 16, lanes].astype(F32)
                sums[i] = sums[i] + (c * c + d * d) * weight
    return y, jnp.concatenate(sums, 0)


def own_kernel(nears, pairs, x_ref, cos_ref, sin_ref, y_ref, diagonal_ref, real_lhs, swap_lhs, power):
    y_ref[...], diagonal_ref[...] = project(nears, pairs, 0, x_ref, cos_ref, sin_ref, real_lhs, swap_lhs, power)


def other_kernel(
    nears, pairs, x_ref, cos_ref, sin_ref, y_ref, diagonal_ref, out_ref, real_lhs, swap_lhs, power
):
    y, diagonal = project(nears, pairs, 1, x_ref, cos_ref, sin_ref, real_lhs, swap_lhs, power)
    y = y + y_ref[...]
    value = y * y
    diagonal = diagonal + diagonal_ref[...]
    for block in range(out_ref.shape[1]):
        rows = slice(block * LANES, (block + 1) * LANES)
        line = jnp.sum(value[rows].T, axis=0, keepdims=True) - jnp.sum(diagonal[rows].T, axis=0, keepdims=True)
        out_ref[:, block : block + 1, :] = jnp.broadcast_to(line[None], (out_ref.shape[0], 1, LANES))


def shards(nears, pairs, devices, signal, bins, mic_positions, grid_positions):
    snaps, samples, mics = signal.shape
    total_mics = mic_positions.shape[1]
    points = grid_positions.shape[1]
    half_points = points // 2
    place = jnp.stack([lax.axis_index("near") * pairs + lax.axis_index("pair"), lax.axis_index("core")]).astype(jnp.int32)
    vmem = pl.BlockSpec(memory_space=pltpu.VMEM)
    smem = pl.BlockSpec(memory_space=pltpu.SMEM)
    anywhere = pl.BlockSpec(memory_space=pl.ANY)

    def steer_shape(count):
        return [pltpu.VMEM((count, total_mics), BF16)] * 2

    def in_hbm(array):
        return pltpu.with_memory_space_constraint(array, pltpu.HBM)

    def in_vmem(array):
        return pltpu.with_memory_space_constraint(array, pltpu.VMEM)

    local, cos, sin = pl.pallas_call(
        functools.partial(dft_kernel, pairs),
        in_specs=[smem, anywhere, anywhere, anywhere, anywhere],
        out_specs=[vmem] * 3,
        out_shape=[
            jax.ShapeDtypeStruct((F, 2 * snaps, mics), BF16),
            *steer_shape(half_points),
        ],
        scratch_shapes=[
            pltpu.VMEM((half_points, LANES), BF16),
            pltpu.VMEM((DEPTH, total_mics), BF16),
            pltpu.VMEM((snaps, samples, mics), BF16),
            pltpu.VMEM((2 * F, snaps, mics), F32),
            pltpu.SMEM(bins.shape, jnp.int32),
            pltpu.VMEM(mic_positions.shape, F32),
            pltpu.VMEM(grid_positions.shape, F32),
            pltpu.VMEM((8, total_mics), F32),
            pltpu.SemaphoreType.DMA((3,)),
            pltpu.SemaphoreType.DMA((snaps,)),
        ],
        compiler_params=pltpu.CompilerParams(vmem_limit_bytes=24 * 2**20),
        name="dft_and_steering",
    )(place, in_hbm(bins), in_hbm(mic_positions), in_hbm(grid_positions), in_hbm(signal))
    own = lax.all_to_all(local, ("near", "pair"), 0, 0, tiled=True)
    other = lax.ppermute(own, "core", [(0, 1), (1, 0)])
    wide = nears * 2 * snaps
    side_mics = total_mics // 2
    scratch = [
        pltpu.VMEM((wide, side_mics), BF16),
        pltpu.VMEM((wide, side_mics), BF16),
        pltpu.VMEM((8, side_mics), F32),
    ]
    steer = (in_vmem(cos), in_vmem(sin))
    cost = pl.CostEstimate(
        flops=4 * half_points * wide * side_mics, bytes_accessed=4 * half_points * side_mics, transcendentals=0
    )
    y, diagonal = pl.pallas_call(
        functools.partial(own_kernel, nears, pairs),
        in_specs=[vmem] * 3,
        out_specs=[vmem] * 2,
        out_shape=[pltpu.VMEM((half_points, wide), F32), pltpu.VMEM((half_points, LANES), F32)],
        scratch_shapes=scratch,
        compiler_params=pltpu.CompilerParams(vmem_limit_bytes=8 * 2**20),
        cost_estimate=cost,
        name="own_projection",
    )(own, *steer)
    mine = pl.pallas_call(
        functools.partial(other_kernel, nears, pairs),
        in_specs=[vmem] * 5,
        out_specs=vmem,
        out_shape=jax.ShapeDtypeStruct((devices, half_points // LANES, LANES), F32),
        scratch_shapes=scratch,
        compiler_params=pltpu.CompilerParams(vmem_limit_bytes=8 * 2**20),
        cost_estimate=cost,
        name="other_projection",
    )(other, *steer, in_vmem(y), in_vmem(diagonal))
    axes = ("wide", "near", "pair", "core")
    everyone = lax.all_to_all(mine, axes, 0, 0, tiled=True)
    summed = jnp.sum(everyone.reshape(-1, F, points), axis=0)
    all_snaps = snaps * lax.axis_size("wide") * nears
    return summed * (1.0 / (math.sqrt(all_snaps) * total_mics))


def solution(mesh):
    groups, inner = mesh.shape["grp"], mesh.shape["inner"]
    pairs = inner // 2
    nears = F // pairs
    fine = Mesh(mesh.devices.reshape(groups // nears, nears, pairs, 2), ("wide", "near", "pair", "core"))
    in_specs = (P(("wide", "near"), None, ("pair", "core")), P(), P(), P())
    step = functools.partial(shards, nears, pairs, groups * inner)
    return jax.shard_map(step, mesh=fine, in_specs=in_specs, out_specs=P(), check_vma=False)
```

```python
import functools
import math

import jax
import jax.numpy as jnp
from jax import lax
from jax.experimental import pallas as pl
from jax.experimental.pallas import tpu as pltpu
from jax.sharding import Mesh, PartitionSpec as P

F = 8
TWO_PI = 2.0 * math.pi
RATE_OVER_SOUND = 51200.0 / 343.0
F32 = jnp.float32
BF16 = jnp.bfloat16
ROUNDER = 12582912.0
LANES = 128
DEPTH = 64
STEP = 512
COLUMNS = 256

SIN_HALF = (4.441535724093539, -7.264680926673255, 3.25204996020452)
COS_HALF = (1.414204080247352, -6.9776420363098905, 5.715238127798347, -1.7283478206531864)
SIN_FINE = (4.442882937668975, -7.308249445082402, 3.6064748105185624, -0.8474638068718637, 0.11600967661123661, -0.009900200019037797)
COS_FINE = (1.4142135623720369, -6.978864199223495, 5.739885708320473, -1.8883460768140574, 0.33280043358005373, -0.036453250292718266, 0.0026021832760962107)


def polynomial(coefs, u):
    value = coefs[-1] * u + coefs[-2]
    for c in coefs[-3::-1]:
        value = value * u + c
    return value


def cos_sin(turns, sin_half=SIN_HALF, cos_half=COS_HALF):
    r = turns - ((turns + ROUNDER) - ROUNDER)
    u = r * r
    s = polynomial(sin_half, u) * r
    c = polynomial(cos_half, u)
    return c * c - 1.0, s * c


def dft_table(bins_ref, samples):
    shape = (F, samples)
    row = lax.broadcasted_iota(jnp.int32, shape, 0)
    ticks = lax.broadcasted_iota(jnp.int32, shape, 1)
    bins = jnp.zeros(shape, jnp.int32)
    for f in range(F):
        bins = jnp.where(row == f, bins_ref[f], bins)
    turns = ((bins * ticks) & (samples - 1)).astype(F32) * (1.0 / samples)
    half = ticks.astype(F32) * (1.0 / samples)
    half = half - ((half + ROUNDER) - ROUNDER)
    half_sin = polynomial(SIN_FINE, half * half) * half
    window = 0.5 * half_sin * half_sin * math.sqrt(8.0 / (3.0 * samples))
    cos, sin = cos_sin(turns, SIN_FINE, COS_FINE)
    return jnp.concatenate([window * cos, -window * sin], 0).astype(BF16)


def split(value):
    high = value.astype(BF16).astype(F32)
    rest = value - high
    middle = rest.astype(BF16).astype(F32)
    return high, middle, rest - middle


def pairs_of(groups):
    return [jnp.concatenate([groups[i], groups[i + 1]], 0) for i in range(0, len(groups), 2)]


def distance_factors(scale, mic_ref, order, grid_ref, grid_start, rows8, left_ref, right_ref):
    at = 0
    for start, width in order:
        near = (1.0 - mic_ref[:, pl.ds(pl.multiple_of(start, LANES), width)]) * scale
        rows8[0:3, at : at + width] = near + near
        rows8[3:4, at : at + width] = jnp.sum(near * near, axis=0, keepdims=True)
        at += width
    rows8[4:5, :] = jnp.ones((1, at), F32)
    rows8[5:8, :] = jnp.zeros((3, at), F32)
    high, middle, low = split(rows8[...])
    for i, rows in enumerate(pairs_of([high, middle, low, high, middle, low, high, middle])):
        right_ref[16 * i : 16 * i + 16, :] = rows.astype(BF16)
    points = left_ref.shape[0]
    far = (grid_ref[:, pl.ds(pl.multiple_of(grid_start, LANES), points)] - 1.0) * scale
    rows8[0:3, :points] = far
    rows8[3:4, :points] = jnp.ones((1, points), F32)
    rows8[4:5, :points] = jnp.sum(far * far, axis=0, keepdims=True) + 1e-30
    high, middle, low = split(rows8[:, :points])
    groups = [high, high, high, middle, middle, middle, low, low]
    zeros = jnp.zeros((LANES - DEPTH, points), F32)
    left_ref[...] = jnp.concatenate(groups + [zeros], 0).T.astype(BF16)


def steer_block(row, row_end, at, width, left_ref, right_ref, cos_ref, sin_ref):
    lanes = slice(at, at + width)
    square = jnp.dot(left_ref[row:row_end, 0:DEPTH], right_ref[0:DEPTH, lanes], preferred_element_type=F32)
    cos, sin = cos_sin(square * lax.rsqrt(square))
    cos_ref[row:row_end, lanes] = cos.astype(BF16)
    sin_ref[row:row_end, lanes] = sin.astype(BF16)


def stages(snaps, points):
    first = max(points * 5 // 16 // 16 * 16, 16)
    second = first + (points - first) // 32 * 16
    return [(0, first), (snaps // 2, second), (snaps, points)]


def interleaved(left, right):
    count = max(len(left), len(right))
    for i in range(count):
        yield tuple(work[i * len(work) // count : (i + 1) * len(work) // count] for work in (left, right))


def mic_order(pairs, width, core):
    return [((2 * pair + lax.rem(core + h, 2)) * width, width) for h in range(2) for pair in range(pairs)]


def dft_kernel(
    pairs, place_ref, bins_hbm, mic_hbm, grid_hbm, signal_ref,
    out_ref, cos_ref, sin_ref, left_ref, right_ref,
    held, total, bins_ref, mic_ref, grid_ref, rows8, small_sem, sem,
):
    snaps, samples, mics = held.shape
    small = [
        pltpu.make_async_copy(source, target, small_sem.at[i])
        for i, (source, target) in enumerate([(bins_hbm, bins_ref), (mic_hbm, mic_ref), (grid_hbm, grid_ref)])
    ]

    def copy(s):
        return pltpu.make_async_copy(signal_ref.at[s], held.at[s], sem.at[s])

    for c in small:
        c.start()
    for s in range(snaps):
        copy(s).start(priority=1)
    for c in small:
        c.wait()
    index, core = place_ref[0], place_ref[1]
    scale = bins_ref[index].astype(F32) * (RATE_OVER_SOUND / samples)
    order = mic_order(pairs, mics, core)
    distance_factors(scale, mic_ref, order, grid_ref, core * (grid_ref.shape[1] // 2), rows8, left_ref, right_ref)
    table = dft_table(bins_ref, samples)

    def transform(s, at, width):
        across = slice(at, at + width)
        total[:, s : s + 1, across] = jnp.dot(table, held[s, :, across], preferred_element_type=F32)[:, None, :]

    columns = min(COLUMNS, mics)
    points, lanes = cos_ref.shape
    step = min(STEP, lanes)
    row = snap = 0
    for snap_end, row_end in stages(snaps, points):
        for s in range(snap, snap_end):
            copy(s).wait()
        transforms = [(s, at, columns) for s in range(snap, snap_end) for at in range(0, mics, columns)]
        steerings = [(row, row_end, at, step) for at in range(0, lanes, step)]
        for take_transforms, take_steerings in interleaved(transforms, steerings):
            for args in take_transforms:
                transform(*args)
            for args in take_steerings:
                steer_block(*args, left_ref, right_ref, cos_ref, sin_ref)
        row, snap = row_end, snap_end
    for f in range(F):
        out_ref[f] = jnp.concatenate([total[f], total[F + f]], 0).astype(BF16)


def project(nears, pairs, side, x_ref, cos_ref, sin_ref, real_lhs, swap_lhs, power):
    blocks, rows, mics = x_ref.shape
    half = rows // 2
    for pair in range(pairs):
        lanes = slice(pair * mics, (pair + 1) * mics)
        squares = jnp.zeros((half, mics), F32)
        for near in range(nears):
            block = x_ref[near * pairs + pair]
            real_lhs[near * rows : (near + 1) * rows, lanes] = block
            block = block.astype(F32)
            top, low = block[:half], block[half:]
            swap_lhs[near * rows : (near + 1) * rows, lanes] = jnp.concatenate([-low, top], 0).astype(BF16)
            squares = squares + (top * top + low * low)
        power[:, lanes] = jnp.broadcast_to(jnp.sum(squares, axis=0, keepdims=True), (8, mics))
    width = pairs * mics
    first = side * width
    form = (((1,), (1,)), ((), ()))
    step = min(COLUMNS, width)
    points = cos_ref.shape[0]
    y = jnp.zeros((points, real_lhs.shape[0]), F32)
    diagonal = jnp.zeros((points, LANES), F32)
    for at in range(0, width, step):
        here = slice(at, at + step)
        cos = cos_ref[:, first + at : first + at + step]
        sin = sin_ref[:, first + at : first + at + step]
        y = y + lax.dot_general(cos, real_lhs[:, here], form, preferred_element_type=F32)
        y = y + lax.dot_general(sin, swap_lhs[:, here], form, preferred_element_type=F32)
        cos = cos.astype(F32)
        sin = sin.astype(F32)
        weighted = (cos * cos + sin * sin) * power[0:1, here]
        for lane in range(0, step, LANES):
            diagonal = diagonal + weighted[:, lane : lane + LANES]
    return y, diagonal


def own_kernel(nears, pairs, x_ref, cos_ref, sin_ref, y_ref, diagonal_ref, real_lhs, swap_lhs, power):
    y_ref[...], diagonal_ref[...] = project(nears, pairs, 0, x_ref, cos_ref, sin_ref, real_lhs, swap_lhs, power)


def other_kernel(
    nears, pairs, x_ref, cos_ref, sin_ref, y_ref, diagonal_ref, out_ref, real_lhs, swap_lhs, power
):
    y, diagonal = project(nears, pairs, 1, x_ref, cos_ref, sin_ref, real_lhs, swap_lhs, power)
    y = y + y_ref[...]
    value = y * y
    diagonal = diagonal + diagonal_ref[...]
    for block in range(out_ref.shape[1]):
        rows = slice(block * LANES, (block + 1) * LANES)
        line = jnp.sum(value[rows].T, axis=0, keepdims=True) - jnp.sum(diagonal[rows].T, axis=0, keepdims=True)
        out_ref[:, block : block + 1, :] = jnp.broadcast_to(line[None], (out_ref.shape[0], 1, LANES))


def shards(nears, pairs, devices, signal, bins, mic_positions, grid_positions):
    snaps, samples, mics = signal.shape
    total_mics = mic_positions.shape[1]
    points = grid_positions.shape[1]
    half_points = points // 2
    place = jnp.stack([lax.axis_index("near") * pairs + lax.axis_index("pair"), lax.axis_index("core")]).astype(jnp.int32)
    vmem = pl.BlockSpec(memory_space=pltpu.VMEM)
    smem = pl.BlockSpec(memory_space=pltpu.SMEM)
    anywhere = pl.BlockSpec(memory_space=pl.ANY)

    def steer_shape(count):
        return [pltpu.VMEM((count, total_mics), BF16)] * 2

    def in_hbm(array):
        return pltpu.with_memory_space_constraint(array, pltpu.HBM)

    def in_vmem(array):
        return pltpu.with_memory_space_constraint(array, pltpu.VMEM)

    local, cos, sin = pl.pallas_call(
        functools.partial(dft_kernel, pairs),
        in_specs=[smem, anywhere, anywhere, anywhere, anywhere],
        out_specs=[vmem] * 3,
        out_shape=[
            jax.ShapeDtypeStruct((F, 2 * snaps, mics), BF16),
            *steer_shape(half_points),
        ],
        scratch_shapes=[
            pltpu.VMEM((half_points, LANES), BF16),
            pltpu.VMEM((DEPTH, total_mics), BF16),
            pltpu.VMEM((snaps, samples, mics), BF16),
            pltpu.VMEM((2 * F, snaps, mics), F32),
            pltpu.SMEM(bins.shape, jnp.int32),
            pltpu.VMEM(mic_positions.shape, F32),
            pltpu.VMEM(grid_positions.shape, F32),
            pltpu.VMEM((8, total_mics), F32),
            pltpu.SemaphoreType.DMA((3,)),
            pltpu.SemaphoreType.DMA((snaps,)),
        ],
        compiler_params=pltpu.CompilerParams(vmem_limit_bytes=24 * 2**20),
        name="dft_and_steering",
    )(place, in_hbm(bins), in_hbm(mic_positions), in_hbm(grid_positions), in_hbm(signal))
    own = lax.all_to_all(local, ("near", "pair"), 0, 0, tiled=True)
    other = lax.ppermute(own, "core", [(0, 1), (1, 0)])
    wide = nears * 2 * snaps
    side_mics = total_mics // 2
    scratch = [
        pltpu.VMEM((wide, side_mics), BF16),
        pltpu.VMEM((wide, side_mics), BF16),
        pltpu.VMEM((8, side_mics), F32),
    ]
    steer = (in_vmem(cos), in_vmem(sin))
    cost = pl.CostEstimate(
        flops=4 * half_points * wide * side_mics, bytes_accessed=4 * half_points * side_mics, transcendentals=0
    )
    y, diagonal = pl.pallas_call(
        functools.partial(own_kernel, nears, pairs),
        in_specs=[vmem] * 3,
        out_specs=[vmem] * 2,
        out_shape=[pltpu.VMEM((half_points, wide), F32), pltpu.VMEM((half_points, LANES), F32)],
        scratch_shapes=scratch,
        compiler_params=pltpu.CompilerParams(vmem_limit_bytes=8 * 2**20),
        cost_estimate=cost,
        name="own_projection",
    )(own, *steer)
    mine = pl.pallas_call(
        functools.partial(other_kernel, nears, pairs),
        in_specs=[vmem] * 5,
        out_specs=vmem,
        out_shape=jax.ShapeDtypeStruct((devices, half_points // LANES, LANES), F32),
        scratch_shapes=scratch,
        compiler_params=pltpu.CompilerParams(vmem_limit_bytes=8 * 2**20),
        cost_estimate=cost,
        name="other_projection",
    )(other, *steer, in_vmem(y), in_vmem(diagonal))
    axes = ("wide", "near", "pair", "core")
    everyone = lax.all_to_all(mine, axes, 0, 0, tiled=True)
    summed = jnp.sum(everyone.reshape(-1, F, points), axis=0)
    all_snaps = snaps * lax.axis_size("wide") * nears
    return summed * (1.0 / (math.sqrt(all_snaps) * total_mics))


def solution(mesh):
    groups, inner = mesh.shape["grp"], mesh.shape["inner"]
    pairs = inner // 2
    nears = F // pairs
    fine = Mesh(mesh.devices.reshape(groups // nears, nears, pairs, 2), ("wide", "near", "pair", "core"))
    in_specs = (P(("wide", "near"), None, ("pair", "core")), P(), P(), P())
    step = functools.partial(shards, nears, pairs, groups * inner)
    return jax.shard_map(step, mesh=fine, in_specs=in_specs, out_specs=P(), check_vma=False)
```

```python
import functools
import math

import jax
import jax.numpy as jnp
from jax import lax
from jax.experimental import pallas as pl
from jax.experimental.pallas import tpu as pltpu
from jax.sharding import Mesh, PartitionSpec as P

F = 8
TWO_PI = 2.0 * math.pi
RATE_OVER_SOUND = 51200.0 / 343.0
F32 = jnp.float32
BF16 = jnp.bfloat16
LANES = 128
DEPTH = 64
STEP = 512
COLUMNS = 256

SIN_HALF = (4.441535724093539, -7.264680926673255, 3.25204996020452)
COS_HALF = (1.414204080247352, -6.9776420363098905, 5.715238127798347, -1.7283478206531864)
SIN_FINE = (4.442882937668975, -7.308249445082402, 3.6064748105185624, -0.8474638068718637, 0.11600967661123661, -0.009900200019037797)
COS_FINE = (1.4142135623720369, -6.978864199223495, 5.739885708320473, -1.8883460768140574, 0.33280043358005373, -0.036453250292718266, 0.0026021832760962107)


def polynomial(coefs, u):
    value = coefs[-1] * u + coefs[-2]
    for c in coefs[-3::-1]:
        value = value * u + c
    return value


def cos_sin(turns, sin_half=SIN_HALF, cos_half=COS_HALF):
    r = turns - jnp.round(turns)
    u = r * r
    s = polynomial(sin_half, u) * r
    c = polynomial(cos_half, u)
    return c * c - 1.0, s * c


def dft_table(bins_ref, samples):
    shape = (F, samples)
    row = lax.broadcasted_iota(jnp.int32, shape, 0)
    ticks = lax.broadcasted_iota(jnp.int32, shape, 1)
    bins = jnp.zeros(shape, jnp.int32)
    for f in range(F):
        bins = jnp.where(row == f, bins_ref[f], bins)
    turns = ((bins * ticks) & (samples - 1)).astype(F32) * (1.0 / samples)
    half = ticks.astype(F32) * (1.0 / samples)
    half = half - jnp.round(half)
    half_sin = polynomial(SIN_FINE, half * half) * half
    window = 0.5 * half_sin * half_sin * math.sqrt(8.0 / (3.0 * samples))
    cos, sin = cos_sin(turns, SIN_FINE, COS_FINE)
    return jnp.concatenate([window * cos, -window * sin], 0).astype(BF16)


def split(value):
    high = value.astype(BF16).astype(F32)
    rest = value - high
    middle = rest.astype(BF16).astype(F32)
    return high, middle, rest - middle


def pairs_of(groups):
    return [jnp.concatenate([groups[i], groups[i + 1]], 0) for i in range(0, len(groups), 2)]


def distance_factors(scale, mic_ref, order, grid_ref, grid_start, rows8, left_ref, right_ref):
    at = 0
    for start, width in order:
        near = (1.0 - mic_ref[:, pl.ds(pl.multiple_of(start, LANES), width)]) * scale
        rows8[0:3, at : at + width] = near + near
        rows8[3:4, at : at + width] = jnp.sum(near * near, axis=0, keepdims=True)
        at += width
    rows8[4:5, :] = jnp.ones((1, at), F32)
    rows8[5:8, :] = jnp.zeros((3, at), F32)
    high, middle, low = split(rows8[...])
    for i, rows in enumerate(pairs_of([high, middle, low, high, middle, low, high, middle])):
        right_ref[16 * i : 16 * i + 16, :] = rows.astype(BF16)
    points = left_ref.shape[0]
    far = (grid_ref[:, pl.ds(pl.multiple_of(grid_start, LANES), points)] - 1.0) * scale
    rows8[0:3, :points] = far
    rows8[3:4, :points] = jnp.ones((1, points), F32)
    rows8[4:5, :points] = jnp.sum(far * far, axis=0, keepdims=True) + 1e-30
    high, middle, low = split(rows8[:, :points])
    groups = [high, high, high, middle, middle, middle, low, low]
    zeros = jnp.zeros((LANES - DEPTH, points), F32)
    left_ref[...] = jnp.concatenate(groups + [zeros], 0).T.astype(BF16)


def steer_block(row, row_end, at, width, left_ref, right_ref, cos_ref, sin_ref):
    lanes = slice(at, at + width)
    square = jnp.dot(left_ref[row:row_end, 0:DEPTH], right_ref[0:DEPTH, lanes], preferred_element_type=F32)
    cos, sin = cos_sin(square * lax.rsqrt(square))
    cos_ref[row:row_end, lanes] = cos.astype(BF16)
    sin_ref[row:row_end, lanes] = sin.astype(BF16)


def stages(snaps, points):
    count = 4
    first = points // 4
    yield 0, first
    for stage in range(1, count + 1):
        row_end = first + (points - first) // 16 * stage // count * 16
        yield snaps * stage // count, points if stage == count else row_end


def interleaved(left, right):
    count = max(len(left), len(right))
    for i in range(count):
        yield tuple(work[i * len(work) // count : (i + 1) * len(work) // count] for work in (left, right))


def mic_order(pairs, width, core):
    return [((2 * pair + lax.rem(core + h, 2)) * width, width) for h in range(2) for pair in range(pairs)]


def dft_kernel(
    pairs, place_ref, bins_hbm, mic_hbm, grid_hbm, signal_ref,
    out_ref, cos_ref, sin_ref, left_ref, right_ref,
    held, total, bins_ref, mic_ref, grid_ref, rows8, small_sem, sem,
):
    snaps, samples, mics = held.shape
    small = [
        pltpu.make_async_copy(source, target, small_sem.at[i])
        for i, (source, target) in enumerate([(bins_hbm, bins_ref), (mic_hbm, mic_ref), (grid_hbm, grid_ref)])
    ]

    def copy(s):
        return pltpu.make_async_copy(signal_ref.at[s], held.at[s], sem.at[s])

    for c in small:
        c.start()
    for s in range(snaps):
        copy(s).start(priority=1)
    for c in small:
        c.wait()
    index, core = place_ref[0], place_ref[1]
    scale = bins_ref[index].astype(F32) * (RATE_OVER_SOUND / samples)
    order = mic_order(pairs, mics, core)
    distance_factors(scale, mic_ref, order, grid_ref, core * (grid_ref.shape[1] // 2), rows8, left_ref, right_ref)
    table = dft_table(bins_ref, samples)

    def transform(s, at, width):
        across = slice(at, at + width)
        total[:, s : s + 1, across] = jnp.dot(table, held[s, :, across], preferred_element_type=F32)[:, None, :]

    columns = min(COLUMNS, mics)
    points, lanes = cos_ref.shape
    step = min(STEP, lanes)
    row = snap = 0
    for snap_end, row_end in stages(snaps, points):
        for s in range(snap, snap_end):
            copy(s).wait()
        transforms = [(s, at, columns) for s in range(snap, snap_end) for at in range(0, mics, columns)]
        steerings = [(row, row_end, at, step) for at in range(0, lanes, step)]
        for take_transforms, take_steerings in interleaved(transforms, steerings):
            for args in take_transforms:
                transform(*args)
            for args in take_steerings:
                steer_block(*args, left_ref, right_ref, cos_ref, sin_ref)
        row, snap = row_end, snap_end
    for f in range(F):
        out_ref[f] = jnp.concatenate([total[f], total[F + f]], 0).astype(BF16)


def project(nears, pairs, side, x_ref, cos_ref, sin_ref, real_lhs, swap_lhs, power):
    blocks, rows, mics = x_ref.shape
    half = rows // 2
    for pair in range(pairs):
        lanes = slice(pair * mics, (pair + 1) * mics)
        squares = jnp.zeros((half, mics), F32)
        for near in range(nears):
            block = x_ref[near * pairs + pair]
            real_lhs[near * rows : (near + 1) * rows, lanes] = block
            block = block.astype(F32)
            top, low = block[:half], block[half:]
            swap_lhs[near * rows : (near + 1) * rows, lanes] = jnp.concatenate([-low, top], 0).astype(BF16)
            squares = squares + (top * top + low * low)
        power[:, lanes] = jnp.broadcast_to(jnp.sum(squares, axis=0, keepdims=True), (8, mics))
    width = pairs * mics
    first = side * width
    form = (((1,), (1,)), ((), ()))
    step = min(COLUMNS, width)
    points = cos_ref.shape[0]
    y = jnp.zeros((points, real_lhs.shape[0]), F32)
    diagonal = jnp.zeros((points, LANES), F32)
    for at in range(0, width, step):
        here = slice(at, at + step)
        cos = cos_ref[:, first + at : first + at + step]
        sin = sin_ref[:, first + at : first + at + step]
        y = y + lax.dot_general(cos, real_lhs[:, here], form, preferred_element_type=F32)
        y = y + lax.dot_general(sin, swap_lhs[:, here], form, preferred_element_type=F32)
        cos = cos.astype(F32)
        sin = sin.astype(F32)
        weighted = (cos * cos + sin * sin) * power[0:1, here]
        for lane in range(0, step, LANES):
            diagonal = diagonal + weighted[:, lane : lane + LANES]
    return y, diagonal


def own_kernel(nears, pairs, x_ref, cos_ref, sin_ref, y_ref, diagonal_ref, real_lhs, swap_lhs, power):
    y_ref[...], diagonal_ref[...] = project(nears, pairs, 0, x_ref, cos_ref, sin_ref, real_lhs, swap_lhs, power)


def other_kernel(
    nears, pairs, x_ref, cos_ref, sin_ref, y_ref, diagonal_ref, out_ref, real_lhs, swap_lhs, power
):
    y, diagonal = project(nears, pairs, 1, x_ref, cos_ref, sin_ref, real_lhs, swap_lhs, power)
    y = y + y_ref[...]
    value = y * y
    diagonal = diagonal + diagonal_ref[...]
    for block in range(out_ref.shape[1]):
        rows = slice(block * LANES, (block + 1) * LANES)
        line = jnp.sum(value[rows].T, axis=0, keepdims=True) - jnp.sum(diagonal[rows].T, axis=0, keepdims=True)
        out_ref[:, block : block + 1, :] = jnp.broadcast_to(line[None], (out_ref.shape[0], 1, LANES))


def shards(nears, pairs, devices, signal, bins, mic_positions, grid_positions):
    snaps, samples, mics = signal.shape
    total_mics = mic_positions.shape[1]
    points = grid_positions.shape[1]
    half_points = points // 2
    place = jnp.stack([lax.axis_index("near") * pairs + lax.axis_index("pair"), lax.axis_index("core")]).astype(jnp.int32)
    vmem = pl.BlockSpec(memory_space=pltpu.VMEM)
    smem = pl.BlockSpec(memory_space=pltpu.SMEM)
    anywhere = pl.BlockSpec(memory_space=pl.ANY)

    def steer_shape(count):
        return [pltpu.VMEM((count, total_mics), BF16)] * 2

    def in_hbm(array):
        return pltpu.with_memory_space_constraint(array, pltpu.HBM)

    def in_vmem(array):
        return pltpu.with_memory_space_constraint(array, pltpu.VMEM)

    local, cos, sin = pl.pallas_call(
        functools.partial(dft_kernel, pairs),
        in_specs=[smem, anywhere, anywhere, anywhere, anywhere],
        out_specs=[vmem] * 3,
        out_shape=[
            jax.ShapeDtypeStruct((F, 2 * snaps, mics), BF16),
            *steer_shape(half_points),
        ],
        scratch_shapes=[
            pltpu.VMEM((half_points, LANES), BF16),
            pltpu.VMEM((DEPTH, total_mics), BF16),
            pltpu.VMEM((snaps, samples, mics), BF16),
            pltpu.VMEM((2 * F, snaps, mics), F32),
            pltpu.SMEM(bins.shape, jnp.int32),
            pltpu.VMEM(mic_positions.shape, F32),
            pltpu.VMEM(grid_positions.shape, F32),
            pltpu.VMEM((8, total_mics), F32),
            pltpu.SemaphoreType.DMA((3,)),
            pltpu.SemaphoreType.DMA((snaps,)),
        ],
        compiler_params=pltpu.CompilerParams(vmem_limit_bytes=24 * 2**20),
        name="dft_and_steering",
    )(place, in_hbm(bins), in_hbm(mic_positions), in_hbm(grid_positions), in_hbm(signal))
    own = lax.all_to_all(local, ("near", "pair"), 0, 0, tiled=True)
    other = lax.ppermute(own, "core", [(0, 1), (1, 0)])
    wide = nears * 2 * snaps
    side_mics = total_mics // 2
    scratch = [
        pltpu.VMEM((wide, side_mics), BF16),
        pltpu.VMEM((wide, side_mics), BF16),
        pltpu.VMEM((8, side_mics), F32),
    ]
    steer = (in_vmem(cos), in_vmem(sin))
    cost = pl.CostEstimate(
        flops=4 * half_points * wide * side_mics, bytes_accessed=4 * half_points * side_mics, transcendentals=0
    )
    y, diagonal = pl.pallas_call(
        functools.partial(own_kernel, nears, pairs),
        in_specs=[vmem] * 3,
        out_specs=[vmem] * 2,
        out_shape=[pltpu.VMEM((half_points, wide), F32), pltpu.VMEM((half_points, LANES), F32)],
        scratch_shapes=scratch,
        compiler_params=pltpu.CompilerParams(vmem_limit_bytes=8 * 2**20),
        cost_estimate=cost,
        name="own_projection",
    )(own, *steer)
    mine = pl.pallas_call(
        functools.partial(other_kernel, nears, pairs),
        in_specs=[vmem] * 5,
        out_specs=vmem,
        out_shape=jax.ShapeDtypeStruct((devices, half_points // LANES, LANES), F32),
        scratch_shapes=scratch,
        compiler_params=pltpu.CompilerParams(vmem_limit_bytes=8 * 2**20),
        cost_estimate=cost,
        name="other_projection",
    )(other, *steer, in_vmem(y), in_vmem(diagonal))
    axes = ("wide", "near", "pair", "core")
    everyone = lax.all_to_all(mine, axes, 0, 0, tiled=True)
    summed = jnp.sum(everyone.reshape(-1, F, points), axis=0)
    all_snaps = snaps * lax.axis_size("wide") * nears
    return summed * (1.0 / (math.sqrt(all_snaps) * total_mics))


def solution(mesh):
    groups, inner = mesh.shape["grp"], mesh.shape["inner"]
    pairs = inner // 2
    nears = F // pairs
    fine = Mesh(mesh.devices.reshape(groups // nears, nears, pairs, 2), ("wide", "near", "pair", "core"))
    in_specs = (P(("wide", "near"), None, ("pair", "core")), P(), P(), P())
    step = functools.partial(shards, nears, pairs, groups * inner)
    return jax.shard_map(step, mesh=fine, in_specs=in_specs, out_specs=P(), check_vma=False)
```

```python
import functools
import math

import jax
import jax.numpy as jnp
from jax import lax
from jax.experimental import pallas as pl
from jax.experimental.pallas import tpu as pltpu
from jax.sharding import Mesh, PartitionSpec as P

F = 8
TWO_PI = 2.0 * math.pi
RATE_OVER_SOUND = 51200.0 / 343.0
F32 = jnp.float32
BF16 = jnp.bfloat16
LANES = 128
DEPTH = 64
STEP = 512
COLUMNS = 256

SIN_HALF = (4.441535724093539, -7.264680926673255, 3.25204996020452)
COS_HALF = (1.414204080247352, -6.9776420363098905, 5.715238127798347, -1.7283478206531864)
SIN_FINE = (4.442882937668975, -7.308249445082402, 3.6064748105185624, -0.8474638068718637, 0.11600967661123661, -0.009900200019037797)
COS_FINE = (1.4142135623720369, -6.978864199223495, 5.739885708320473, -1.8883460768140574, 0.33280043358005373, -0.036453250292718266, 0.0026021832760962107)


def polynomial(coefs, u):
    value = coefs[-1] * u + coefs[-2]
    for c in coefs[-3::-1]:
        value = value * u + c
    return value


def cos_sin(turns, sin_half=SIN_HALF, cos_half=COS_HALF):
    r = turns - jnp.round(turns)
    u = r * r
    s = polynomial(sin_half, u) * r
    c = polynomial(cos_half, u)
    return c * c - 1.0, s * c


def dft_table(bins_ref, samples):
    shape = (F, samples)
    row = lax.broadcasted_iota(jnp.int32, shape, 0)
    ticks = lax.broadcasted_iota(jnp.int32, shape, 1)
    bins = jnp.zeros(shape, jnp.int32)
    for f in range(F):
        bins = jnp.where(row == f, bins_ref[f], bins)
    turns = ((bins * ticks) & (samples - 1)).astype(F32) * (1.0 / samples)
    half = ticks.astype(F32) * (1.0 / samples)
    half = half - jnp.round(half)
    half_sin = polynomial(SIN_FINE, half * half) * half
    window = 0.5 * half_sin * half_sin * math.sqrt(8.0 / (3.0 * samples))
    cos, sin = cos_sin(turns, SIN_FINE, COS_FINE)
    return jnp.concatenate([window * cos, -window * sin], 0).astype(BF16)


def split(value):
    high = value.astype(BF16).astype(F32)
    rest = value - high
    middle = rest.astype(BF16).astype(F32)
    return high, middle, rest - middle


def pairs_of(groups):
    return [jnp.concatenate([groups[i], groups[i + 1]], 0) for i in range(0, len(groups), 2)]


def distance_factors(scale, mic_ref, order, grid_ref, grid_start, rows8, left_ref, right_ref):
    at = 0
    for start, width in order:
        near = (1.0 - mic_ref[:, pl.ds(pl.multiple_of(start, LANES), width)]) * scale
        rows8[0:3, at : at + width] = near + near
        rows8[3:4, at : at + width] = jnp.sum(near * near, axis=0, keepdims=True)
        at += width
    rows8[4:5, :] = jnp.ones((1, at), F32)
    rows8[5:8, :] = jnp.zeros((3, at), F32)
    high, middle, low = split(rows8[...])
    for i, rows in enumerate(pairs_of([high, middle, low, high, middle, low, high, middle])):
        right_ref[16 * i : 16 * i + 16, :] = rows.astype(BF16)
    points = left_ref.shape[0]
    far = (grid_ref[:, pl.ds(pl.multiple_of(grid_start, LANES), points)] - 1.0) * scale
    rows8[0:3, :points] = far
    rows8[3:4, :points] = jnp.ones((1, points), F32)
    rows8[4:5, :points] = jnp.sum(far * far, axis=0, keepdims=True) + 1e-30
    high, middle, low = split(rows8[:, :points])
    groups = [high, high, high, middle, middle, middle, low, low]
    zeros = jnp.zeros((LANES - DEPTH, points), F32)
    left_ref[...] = jnp.concatenate(groups + [zeros], 0).T.astype(BF16)


def steer_block(row, row_end, at, width, left_ref, right_ref, cos_ref, sin_ref):
    lanes = slice(at, at + width)
    square = jnp.dot(left_ref[row:row_end, 0:DEPTH], right_ref[0:DEPTH, lanes], preferred_element_type=F32)
    cos, sin = cos_sin(square * lax.rsqrt(square))
    cos_ref[row:row_end, lanes] = cos.astype(BF16)
    sin_ref[row:row_end, lanes] = sin.astype(BF16)


def stages(snaps, points):
    count = 4
    first = points // 4
    yield 0, first
    for stage in range(1, count + 1):
        row_end = first + (points - first) // 16 * stage // count * 16
        yield snaps * stage // count, points if stage == count else row_end


def interleaved(left, right):
    count = max(len(left), len(right))
    for i in range(count):
        yield tuple(work[i * len(work) // count : (i + 1) * len(work) // count] for work in (left, right))


def mic_order(pairs, width, core):
    return [((2 * pair + lax.rem(core + h, 2)) * width, width) for h in range(2) for pair in range(pairs)]


def dft_kernel(
    pairs, place_ref, bins_hbm, mic_hbm, grid_hbm, signal_ref,
    out_ref, cos_ref, sin_ref, left_ref, right_ref,
    held, total, bins_ref, mic_ref, grid_ref, rows8, small_sem, sem,
):
    snaps, samples, mics = held.shape
    small = [
        pltpu.make_async_copy(source, target, small_sem.at[i])
        for i, (source, target) in enumerate([(bins_hbm, bins_ref), (mic_hbm, mic_ref), (grid_hbm, grid_ref)])
    ]

    def copy(s):
        return pltpu.make_async_copy(signal_ref.at[s], held.at[s], sem.at[s])

    for c in small:
        c.start()
    for s in range(snaps):
        copy(s).start(priority=1)
    for c in small:
        c.wait()
    index, core = place_ref[0], place_ref[1]
    scale = bins_ref[index].astype(F32) * (RATE_OVER_SOUND / samples)
    order = mic_order(pairs, mics, core)
    distance_factors(scale, mic_ref, order, grid_ref, core * (grid_ref.shape[1] // 2), rows8, left_ref, right_ref)
    table = dft_table(bins_ref, samples)

    def transform(s, at, width):
        across = slice(at, at + width)
        total[s, :, across] = jnp.dot(table, held[s, :, across], preferred_element_type=F32)

    columns = min(COLUMNS, mics)
    points, lanes = cos_ref.shape
    step = min(STEP, lanes)
    row = snap = 0
    for snap_end, row_end in stages(snaps, points):
        for s in range(snap, snap_end):
            copy(s).wait()
        transforms = [(s, at, columns) for s in range(snap, snap_end) for at in range(0, mics, columns)]
        steerings = [(row, row_end, at, step) for at in range(0, lanes, step)]
        for take_transforms, take_steerings in interleaved(transforms, steerings):
            for args in take_transforms:
                transform(*args)
            for args in take_steerings:
                steer_block(*args, left_ref, right_ref, cos_ref, sin_ref)
        row, snap = row_end, snap_end
    for at in range(0, mics, columns):
        across = slice(at, at + columns)
        turned = jnp.transpose(total[:, :, across], (1, 0, 2))
        for f in range(F):
            out_ref[f, :, across] = jnp.concatenate([turned[f], turned[F + f]], 0).astype(BF16)


def project(nears, pairs, side, x_ref, cos_ref, sin_ref, real_lhs, swap_lhs, power):
    blocks, rows, mics = x_ref.shape
    half = rows // 2
    for pair in range(pairs):
        lanes = slice(pair * mics, (pair + 1) * mics)
        squares = jnp.zeros((half, mics), F32)
        for near in range(nears):
            block = x_ref[near * pairs + pair]
            real_lhs[near * rows : (near + 1) * rows, lanes] = block
            block = block.astype(F32)
            top, low = block[:half], block[half:]
            swap_lhs[near * rows : (near + 1) * rows, lanes] = jnp.concatenate([-low, top], 0).astype(BF16)
            squares = squares + (top * top + low * low)
        power[:, lanes] = jnp.broadcast_to(jnp.sum(squares, axis=0, keepdims=True), (8, mics))
    width = pairs * mics
    first = side * width
    form = (((1,), (1,)), ((), ()))
    step = min(COLUMNS, width)
    points = cos_ref.shape[0]
    y = jnp.zeros((points, real_lhs.shape[0]), F32)
    diagonal = jnp.zeros((points, LANES), F32)
    for at in range(0, width, step):
        here = slice(at, at + step)
        cos = cos_ref[:, first + at : first + at + step]
        sin = sin_ref[:, first + at : first + at + step]
        y = y + lax.dot_general(cos, real_lhs[:, here], form, preferred_element_type=F32)
        y = y + lax.dot_general(sin, swap_lhs[:, here], form, preferred_element_type=F32)
        cos = cos.astype(F32)
        sin = sin.astype(F32)
        weighted = (cos * cos + sin * sin) * power[0:1, here]
        for lane in range(0, step, LANES):
            diagonal = diagonal + weighted[:, lane : lane + LANES]
    return y, diagonal


def own_kernel(nears, pairs, x_ref, cos_ref, sin_ref, y_ref, diagonal_ref, real_lhs, swap_lhs, power):
    y_ref[...], diagonal_ref[...] = project(nears, pairs, 0, x_ref, cos_ref, sin_ref, real_lhs, swap_lhs, power)


def other_kernel(
    nears, pairs, x_ref, cos_ref, sin_ref, y_ref, diagonal_ref, out_ref, real_lhs, swap_lhs, power
):
    y, diagonal = project(nears, pairs, 1, x_ref, cos_ref, sin_ref, real_lhs, swap_lhs, power)
    y = y + y_ref[...]
    value = y * y
    if value.shape[1] % LANES:
        value = jnp.concatenate([value, jnp.zeros((value.shape[0], -value.shape[1] % LANES), F32)], 1)
    total = -(diagonal + diagonal_ref[...])
    for lane in range(0, value.shape[1], LANES):
        total = total + value[:, lane : lane + LANES]
    for block in range(out_ref.shape[1]):
        line = jnp.sum(total[block * LANES : (block + 1) * LANES].T, axis=0, keepdims=True)
        out_ref[:, block : block + 1, :] = jnp.broadcast_to(line[None], (out_ref.shape[0], 1, LANES))


def shards(nears, pairs, devices, signal, bins, mic_positions, grid_positions):
    snaps, samples, mics = signal.shape
    total_mics = mic_positions.shape[1]
    points = grid_positions.shape[1]
    half_points = points // 2
    place = jnp.stack([lax.axis_index("near") * pairs + lax.axis_index("pair"), lax.axis_index("core")]).astype(jnp.int32)
    vmem = pl.BlockSpec(memory_space=pltpu.VMEM)
    smem = pl.BlockSpec(memory_space=pltpu.SMEM)
    anywhere = pl.BlockSpec(memory_space=pl.ANY)

    def steer_shape(count):
        return [pltpu.VMEM((count, total_mics), BF16)] * 2

    def in_hbm(array):
        return pltpu.with_memory_space_constraint(array, pltpu.HBM)

    def in_vmem(array):
        return pltpu.with_memory_space_constraint(array, pltpu.VMEM)

    local, cos, sin = pl.pallas_call(
        functools.partial(dft_kernel, pairs),
        in_specs=[smem, anywhere, anywhere, anywhere, anywhere],
        out_specs=[vmem] * 3,
        out_shape=[
            jax.ShapeDtypeStruct((F, 2 * snaps, mics), BF16),
            *steer_shape(half_points),
        ],
        scratch_shapes=[
            pltpu.VMEM((half_points, LANES), BF16),
            pltpu.VMEM((DEPTH, total_mics), BF16),
            pltpu.VMEM((snaps, samples, mics), BF16),
            pltpu.VMEM((snaps, 2 * F, mics), F32),
            pltpu.SMEM(bins.shape, jnp.int32),
            pltpu.VMEM(mic_positions.shape, F32),
            pltpu.VMEM(grid_positions.shape, F32),
            pltpu.VMEM((8, total_mics), F32),
            pltpu.SemaphoreType.DMA((3,)),
            pltpu.SemaphoreType.DMA((snaps,)),
        ],
        compiler_params=pltpu.CompilerParams(vmem_limit_bytes=24 * 2**20),
        name="dft_and_steering",
    )(place, in_hbm(bins), in_hbm(mic_positions), in_hbm(grid_positions), in_hbm(signal))
    own = lax.all_to_all(local, ("near", "pair"), 0, 0, tiled=True)
    other = lax.ppermute(own, "core", [(0, 1), (1, 0)])
    wide = nears * 2 * snaps
    side_mics = total_mics // 2
    scratch = [
        pltpu.VMEM((wide, side_mics), BF16),
        pltpu.VMEM((wide, side_mics), BF16),
        pltpu.VMEM((8, side_mics), F32),
    ]
    steer = (in_vmem(cos), in_vmem(sin))
    cost = pl.CostEstimate(
        flops=4 * half_points * wide * side_mics, bytes_accessed=4 * half_points * side_mics, transcendentals=0
    )
    y, diagonal = pl.pallas_call(
        functools.partial(own_kernel, nears, pairs),
        in_specs=[vmem] * 3,
        out_specs=[vmem] * 2,
        out_shape=[pltpu.VMEM((half_points, wide), F32), pltpu.VMEM((half_points, LANES), F32)],
        scratch_shapes=scratch,
        compiler_params=pltpu.CompilerParams(vmem_limit_bytes=8 * 2**20),
        cost_estimate=cost,
        name="own_projection",
    )(own, *steer)
    mine = pl.pallas_call(
        functools.partial(other_kernel, nears, pairs),
        in_specs=[vmem] * 5,
        out_specs=vmem,
        out_shape=jax.ShapeDtypeStruct((devices, half_points // LANES, LANES), F32),
        scratch_shapes=scratch,
        compiler_params=pltpu.CompilerParams(vmem_limit_bytes=8 * 2**20),
        cost_estimate=cost,
        name="other_projection",
    )(other, *steer, in_vmem(y), in_vmem(diagonal))
    axes = ("wide", "near", "pair", "core")
    everyone = lax.all_to_all(mine, axes, 0, 0, tiled=True)
    summed = jnp.sum(everyone.reshape(-1, F, points), axis=0)
    all_snaps = snaps * lax.axis_size("wide") * nears
    return summed * (1.0 / (math.sqrt(all_snaps) * total_mics))


def solution(mesh):
    groups, inner = mesh.shape["grp"], mesh.shape["inner"]
    pairs = inner // 2
    nears = F // pairs
    fine = Mesh(mesh.devices.reshape(groups // nears, nears, pairs, 2), ("wide", "near", "pair", "core"))
    in_specs = (P(("wide", "near"), None, ("pair", "core")), P(), P(), P())
    step = functools.partial(shards, nears, pairs, groups * inner)
    return jax.shard_map(step, mesh=fine, in_specs=in_specs, out_specs=P(), check_vma=False)
```

```python
import functools
import math

import jax
import jax.numpy as jnp
from jax import lax
from jax.experimental import pallas as pl
from jax.experimental.pallas import tpu as pltpu
from jax.sharding import Mesh, PartitionSpec as P

F = 8
TWO_PI = 2.0 * math.pi
RATE_OVER_SOUND = 51200.0 / 343.0
F32 = jnp.float32
BF16 = jnp.bfloat16
LANES = 128
DEPTH = 64
STEP = 512
COLUMNS = 256

SIN_HALF = (4.441535724093539, -7.264680926673255, 3.25204996020452)
COS_HALF = (1.414204080247352, -6.9776420363098905, 5.715238127798347, -1.7283478206531864)
SIN_FINE = (4.442882937668975, -7.308249445082402, 3.6064748105185624, -0.8474638068718637, 0.11600967661123661, -0.009900200019037797)
COS_FINE = (1.4142135623720369, -6.978864199223495, 5.739885708320473, -1.8883460768140574, 0.33280043358005373, -0.036453250292718266, 0.0026021832760962107)


def polynomial(coefs, u):
    value = coefs[-1] * u + coefs[-2]
    for c in coefs[-3::-1]:
        value = value * u + c
    return value


def cos_sin(turns, sin_half=SIN_HALF, cos_half=COS_HALF):
    r = turns - jnp.round(turns)
    u = r * r
    s = polynomial(sin_half, u) * r
    c = polynomial(cos_half, u)
    return c * c - 1.0, s * c


def dft_table(bins_ref, samples):
    shape = (F, samples)
    row = lax.broadcasted_iota(jnp.int32, shape, 0)
    ticks = lax.broadcasted_iota(jnp.int32, shape, 1)
    bins = jnp.zeros(shape, jnp.int32)
    for f in range(F):
        bins = jnp.where(row == f, bins_ref[f], bins)
    turns = ((bins * ticks) & (samples - 1)).astype(F32) * (1.0 / samples)
    half = ticks.astype(F32) * (1.0 / samples)
    half = half - jnp.round(half)
    half_sin = polynomial(SIN_FINE, half * half) * half
    window = 0.5 * half_sin * half_sin * math.sqrt(8.0 / (3.0 * samples))
    cos, sin = cos_sin(turns, SIN_FINE, COS_FINE)
    return jnp.concatenate([window * cos, -window * sin], 0).astype(BF16)


def split(value):
    high = value.astype(BF16).astype(F32)
    rest = value - high
    middle = rest.astype(BF16).astype(F32)
    return high, middle, rest - middle


def pairs_of(groups):
    return [jnp.concatenate([groups[i], groups[i + 1]], 0) for i in range(0, len(groups), 2)]


def distance_factors(scale, mic_ref, order, grid_ref, grid_start, rows8, left_ref, right_ref):
    at = 0
    for start, width in order:
        near = (1.0 - mic_ref[:, pl.ds(pl.multiple_of(start, LANES), width)]) * scale
        rows8[0:3, at : at + width] = near + near
        rows8[3:4, at : at + width] = jnp.sum(near * near, axis=0, keepdims=True)
        at += width
    rows8[4:5, :] = jnp.ones((1, at), F32)
    rows8[5:8, :] = jnp.zeros((3, at), F32)
    high, middle, low = split(rows8[...])
    for i, rows in enumerate(pairs_of([high, middle, low, high, middle, low, high, middle])):
        right_ref[16 * i : 16 * i + 16, :] = rows.astype(BF16)
    points = left_ref.shape[0]
    far = (grid_ref[:, pl.ds(pl.multiple_of(grid_start, LANES), points)] - 1.0) * scale
    rows8[0:3, :points] = far
    rows8[3:4, :points] = jnp.ones((1, points), F32)
    rows8[4:5, :points] = jnp.sum(far * far, axis=0, keepdims=True) + 1e-30
    high, middle, low = split(rows8[:, :points])
    groups = [high, high, high, middle, middle, middle, low, low]
    zeros = jnp.zeros((LANES - DEPTH, points), F32)
    left_ref[...] = jnp.concatenate(groups + [zeros], 0).T.astype(BF16)


def steer_block(row, row_end, at, width, left_ref, right_ref, cos_ref, sin_ref):
    lanes = slice(at, at + width)
    square = jnp.dot(left_ref[row:row_end, 0:DEPTH], right_ref[0:DEPTH, lanes], preferred_element_type=F32)
    cos, sin = cos_sin(square * lax.rsqrt(square))
    cos_ref[row:row_end, lanes] = cos.astype(BF16)
    sin_ref[row:row_end, lanes] = sin.astype(BF16)


def stages(snaps, points):
    count = 4
    first = points // 4
    yield 0, first
    for stage in range(1, count + 1):
        row_end = first + (points - first) // 16 * stage // count * 16
        yield snaps * stage // count, points if stage == count else row_end


def interleaved(left, right):
    count = max(len(left), len(right))
    for i in range(count):
        yield tuple(work[i * len(work) // count : (i + 1) * len(work) // count] for work in (left, right))


def mic_order(pairs, width, core):
    return [((2 * pair + lax.rem(core + h, 2)) * width, width) for h in range(2) for pair in range(pairs)]


def dft_kernel(
    pairs, bins_hbm, mic_hbm, grid_hbm, signal_ref,
    out_ref, cos_ref, sin_ref, left_ref, right_ref,
    held, total, bins_ref, mic_ref, grid_ref, rows8, small_sem, sem,
):
    snaps, samples, mics = held.shape
    small = [
        pltpu.make_async_copy(source, target, small_sem.at[i])
        for i, (source, target) in enumerate([(bins_hbm, bins_ref), (mic_hbm, mic_ref), (grid_hbm, grid_ref)])
    ]

    def copy(s):
        return pltpu.make_async_copy(signal_ref.at[s], held.at[s], sem.at[s])

    for c in small:
        c.start()
    for s in range(snaps):
        copy(s).start(priority=1)
    for c in small:
        c.wait()
    index, core = lax.axis_index("near") * pairs + lax.axis_index("pair"), lax.axis_index("core")
    scale = bins_ref[index].astype(F32) * (RATE_OVER_SOUND / samples)
    order = mic_order(pairs, mics, core)
    distance_factors(scale, mic_ref, order, grid_ref, core * (grid_ref.shape[1] // 2), rows8, left_ref, right_ref)
    table = dft_table(bins_ref, samples)

    def transform(s, at, width):
        across = slice(at, at + width)
        total[s, :, across] = jnp.dot(table, held[s, :, across], preferred_element_type=F32)

    columns = min(COLUMNS, mics)
    points, lanes = cos_ref.shape
    step = min(STEP, lanes)
    row = snap = 0
    for snap_end, row_end in stages(snaps, points):
        for s in range(snap, snap_end):
            copy(s).wait()
        transforms = [(s, at, columns) for s in range(snap, snap_end) for at in range(0, mics, columns)]
        steerings = [(row, row_end, at, step) for at in range(0, lanes, step)]
        for take_transforms, take_steerings in interleaved(transforms, steerings):
            for args in take_transforms:
                transform(*args)
            for args in take_steerings:
                steer_block(*args, left_ref, right_ref, cos_ref, sin_ref)
        row, snap = row_end, snap_end
    for at in range(0, mics, columns):
        across = slice(at, at + columns)
        turned = jnp.transpose(total[:, :, across], (1, 0, 2))
        for f in range(F):
            out_ref[f, :, across] = jnp.concatenate([turned[f], turned[F + f]], 0).astype(BF16)


def project(nears, pairs, side, x_ref, cos_ref, sin_ref, real_lhs, swap_lhs, power):
    blocks, rows, mics = x_ref.shape
    half = rows // 2
    for pair in range(pairs):
        lanes = slice(pair * mics, (pair + 1) * mics)
        squares = jnp.zeros((half, mics), F32)
        for near in range(nears):
            block = x_ref[near * pairs + pair]
            real_lhs[near * rows : (near + 1) * rows, lanes] = block
            block = block.astype(F32)
            top, low = block[:half], block[half:]
            swap_lhs[near * rows : (near + 1) * rows, lanes] = jnp.concatenate([-low, top], 0).astype(BF16)
            squares = squares + (top * top + low * low)
        power[:, lanes] = jnp.broadcast_to(jnp.sum(squares, axis=0, keepdims=True), (8, mics))
    width = pairs * mics
    first = side * width
    form = (((1,), (1,)), ((), ()))
    step = min(COLUMNS, width)
    points = cos_ref.shape[0]
    y = jnp.zeros((points, real_lhs.shape[0]), F32)
    diagonal = jnp.zeros((points, LANES), F32)
    for at in range(0, width, step):
        here = slice(at, at + step)
        cos = cos_ref[:, first + at : first + at + step]
        sin = sin_ref[:, first + at : first + at + step]
        y = y + lax.dot_general(cos, real_lhs[:, here], form, preferred_element_type=F32)
        y = y + lax.dot_general(sin, swap_lhs[:, here], form, preferred_element_type=F32)
        cos = cos.astype(F32)
        sin = sin.astype(F32)
        weighted = (cos * cos + sin * sin) * power[0:1, here]
        for lane in range(0, step, LANES):
            diagonal = diagonal + weighted[:, lane : lane + LANES]
    return y, diagonal


def own_kernel(nears, pairs, x_ref, cos_ref, sin_ref, y_ref, diagonal_ref, real_lhs, swap_lhs, power):
    y_ref[...], diagonal_ref[...] = project(nears, pairs, 0, x_ref, cos_ref, sin_ref, real_lhs, swap_lhs, power)


def other_kernel(
    nears, pairs, x_ref, cos_ref, sin_ref, y_ref, diagonal_ref, out_ref, real_lhs, swap_lhs, power
):
    y, diagonal = project(nears, pairs, 1, x_ref, cos_ref, sin_ref, real_lhs, swap_lhs, power)
    y = y + y_ref[...]
    value = y * y
    if value.shape[1] % LANES:
        value = jnp.concatenate([value, jnp.zeros((value.shape[0], -value.shape[1] % LANES), F32)], 1)
    total = -(diagonal + diagonal_ref[...])
    for lane in range(0, value.shape[1], LANES):
        total = total + value[:, lane : lane + LANES]
    for block in range(out_ref.shape[1]):
        line = jnp.sum(total[block * LANES : (block + 1) * LANES].T, axis=0, keepdims=True)
        out_ref[:, block : block + 1, :] = jnp.broadcast_to(line[None], (out_ref.shape[0], 1, LANES))


def shards(nears, pairs, devices, signal, bins, mic_positions, grid_positions):
    snaps, samples, mics = signal.shape
    total_mics = mic_positions.shape[1]
    points = grid_positions.shape[1]
    half_points = points // 2
    vmem = pl.BlockSpec(memory_space=pltpu.VMEM)
    anywhere = pl.BlockSpec(memory_space=pl.ANY)

    def steer_shape(count):
        return [pltpu.VMEM((count, total_mics), BF16)] * 2

    def in_hbm(array):
        return pltpu.with_memory_space_constraint(array, pltpu.HBM)

    def in_vmem(array):
        return pltpu.with_memory_space_constraint(array, pltpu.VMEM)

    local, cos, sin = pl.pallas_call(
        functools.partial(dft_kernel, pairs),
        in_specs=[anywhere] * 4,
        out_specs=[vmem] * 3,
        out_shape=[
            jax.ShapeDtypeStruct((F, 2 * snaps, mics), BF16),
            *steer_shape(half_points),
        ],
        scratch_shapes=[
            pltpu.VMEM((half_points, LANES), BF16),
            pltpu.VMEM((DEPTH, total_mics), BF16),
            pltpu.VMEM((snaps, samples, mics), BF16),
            pltpu.VMEM((snaps, 2 * F, mics), F32),
            pltpu.SMEM(bins.shape, jnp.int32),
            pltpu.VMEM(mic_positions.shape, F32),
            pltpu.VMEM(grid_positions.shape, F32),
            pltpu.VMEM((8, total_mics), F32),
            pltpu.SemaphoreType.DMA((3,)),
            pltpu.SemaphoreType.DMA((snaps,)),
        ],
        compiler_params=pltpu.CompilerParams(vmem_limit_bytes=24 * 2**20),
        name="dft_and_steering",
    )(in_hbm(bins), in_hbm(mic_positions), in_hbm(grid_positions), in_hbm(signal))
    own = lax.all_to_all(local, ("near", "pair"), 0, 0, tiled=True)
    other = lax.ppermute(own, "core", [(0, 1), (1, 0)])
    wide = nears * 2 * snaps
    side_mics = total_mics // 2
    scratch = [
        pltpu.VMEM((wide, side_mics), BF16),
        pltpu.VMEM((wide, side_mics), BF16),
        pltpu.VMEM((8, side_mics), F32),
    ]
    steer = (in_vmem(cos), in_vmem(sin))
    cost = pl.CostEstimate(
        flops=4 * half_points * wide * side_mics, bytes_accessed=4 * half_points * side_mics, transcendentals=0
    )
    y, diagonal = pl.pallas_call(
        functools.partial(own_kernel, nears, pairs),
        in_specs=[vmem] * 3,
        out_specs=[vmem] * 2,
        out_shape=[pltpu.VMEM((half_points, wide), F32), pltpu.VMEM((half_points, LANES), F32)],
        scratch_shapes=scratch,
        compiler_params=pltpu.CompilerParams(vmem_limit_bytes=8 * 2**20),
        cost_estimate=cost,
        name="own_projection",
    )(own, *steer)
    mine = pl.pallas_call(
        functools.partial(other_kernel, nears, pairs),
        in_specs=[vmem] * 5,
        out_specs=vmem,
        out_shape=jax.ShapeDtypeStruct((devices, half_points // LANES, LANES), F32),
        scratch_shapes=scratch,
        compiler_params=pltpu.CompilerParams(vmem_limit_bytes=8 * 2**20),
        cost_estimate=cost,
        name="other_projection",
    )(other, *steer, in_vmem(y), in_vmem(diagonal))
    axes = ("wide", "near", "pair", "core")
    everyone = lax.all_to_all(mine, axes, 0, 0, tiled=True)
    summed = jnp.sum(everyone.reshape(-1, F, points), axis=0)
    all_snaps = snaps * lax.axis_size("wide") * nears
    return summed * (1.0 / (math.sqrt(all_snaps) * total_mics))


def solution(mesh):
    groups, inner = mesh.shape["grp"], mesh.shape["inner"]
    pairs = inner // 2
    nears = F // pairs
    fine = Mesh(mesh.devices.reshape(groups // nears, nears, pairs, 2), ("wide", "near", "pair", "core"))
    in_specs = (P(("wide", "near"), None, ("pair", "core")), P(), P(), P())
    step = functools.partial(shards, nears, pairs, groups * inner)
    return jax.shard_map(step, mesh=fine, in_specs=in_specs, out_specs=P(), check_vma=False)
```

```python
import functools
import math

import jax
import jax.numpy as jnp
from jax import lax
from jax.experimental import pallas as pl
from jax.experimental.pallas import tpu as pltpu
from jax.sharding import Mesh, PartitionSpec as P

F = 8
TWO_PI = 2.0 * math.pi
RATE_OVER_SOUND = 51200.0 / 343.0
F32 = jnp.float32
BF16 = jnp.bfloat16
LANES = 128
DEPTH = 64
STEP = 512
COLUMNS = 256

SIN_HALF = (4.441535724093539, -7.264680926673255, 3.25204996020452)
COS_HALF = (1.414204080247352, -6.9776420363098905, 5.715238127798347, -1.7283478206531864)
SIN_FINE = (4.442882937668975, -7.308249445082402, 3.6064748105185624, -0.8474638068718637, 0.11600967661123661, -0.009900200019037797)
COS_FINE = (1.4142135623720369, -6.978864199223495, 5.739885708320473, -1.8883460768140574, 0.33280043358005373, -0.036453250292718266, 0.0026021832760962107)


def polynomial(coefs, u):
    value = coefs[-1] * u + coefs[-2]
    for c in coefs[-3::-1]:
        value = value * u + c
    return value


def cos_sin(turns, sin_half=SIN_HALF, cos_half=COS_HALF):
    r = turns - jnp.round(turns)
    u = r * r
    s = polynomial(sin_half, u) * r
    c = polynomial(cos_half, u)
    return c * c - 1.0, s * c


def dft_table(bins_ref, samples):
    shape = (F, samples)
    row = lax.broadcasted_iota(jnp.int32, shape, 0)
    ticks = lax.broadcasted_iota(jnp.int32, shape, 1)
    bins = jnp.zeros(shape, jnp.int32)
    for f in range(F):
        bins = jnp.where(row == f, bins_ref[f], bins)
    turns = ((bins * ticks) & (samples - 1)).astype(F32) * (1.0 / samples)
    half = ticks.astype(F32) * (1.0 / samples)
    half = half - jnp.round(half)
    half_sin = polynomial(SIN_FINE, half * half) * half
    window = 0.5 * half_sin * half_sin * math.sqrt(8.0 / (3.0 * samples))
    cos, sin = cos_sin(turns, SIN_FINE, COS_FINE)
    return jnp.concatenate([window * cos, -window * sin], 0).astype(BF16)


def split(value):
    high = value.astype(BF16).astype(F32)
    rest = value - high
    middle = rest.astype(BF16).astype(F32)
    return high, middle, rest - middle


def pairs_of(groups):
    return [jnp.concatenate([groups[i], groups[i + 1]], 0) for i in range(0, len(groups), 2)]


def distance_factors(scale, mic_ref, order, grid_ref, grid_start, rows8, left_ref, right_ref):
    at = 0
    for start, width in order:
        near = (1.0 - mic_ref[:, pl.ds(pl.multiple_of(start, LANES), width)]) * scale
        rows8[0:3, at : at + width] = near + near
        rows8[3:4, at : at + width] = jnp.sum(near * near, axis=0, keepdims=True)
        at += width
    rows8[4:5, :] = jnp.ones((1, at), F32)
    rows8[5:8, :] = jnp.zeros((3, at), F32)
    high, middle, low = split(rows8[...])
    for i, rows in enumerate(pairs_of([high, middle, low, high, middle, low, high, middle])):
        right_ref[16 * i : 16 * i + 16, :] = rows.astype(BF16)
    points = left_ref.shape[0]
    far = (grid_ref[:, pl.ds(pl.multiple_of(grid_start, LANES), points)] - 1.0) * scale
    rows8[0:3, :points] = far
    rows8[3:4, :points] = jnp.ones((1, points), F32)
    rows8[4:5, :points] = jnp.sum(far * far, axis=0, keepdims=True) + 1e-30
    high, middle, low = split(rows8[:, :points])
    groups = [high, high, high, middle, middle, middle, low, low]
    zeros = jnp.zeros((LANES - DEPTH, points), F32)
    left_ref[...] = jnp.concatenate(groups + [zeros], 0).T.astype(BF16)


def steer_block(row, row_end, at, width, left_ref, right_ref, cos_ref, sin_ref):
    lanes = slice(at, at + width)
    square = jnp.dot(left_ref[row:row_end, 0:DEPTH], right_ref[0:DEPTH, lanes], preferred_element_type=F32)
    cos, sin = cos_sin(square * lax.rsqrt(square))
    cos_ref[row:row_end, lanes] = cos.astype(BF16)
    sin_ref[row:row_end, lanes] = sin.astype(BF16)


def stages(snaps, points):
    count = 4
    first = points // 4
    yield 0, first
    for stage in range(1, count + 1):
        row_end = first + (points - first) // 16 * stage // count * 16
        yield snaps * stage // count, points if stage == count else row_end


def interleaved(left, right):
    count = max(len(left), len(right))
    for i in range(count):
        yield tuple(work[i * len(work) // count : (i + 1) * len(work) // count] for work in (left, right))


def mic_order(pairs, width, core):
    return [((2 * pair + lax.rem(core + h, 2)) * width, width) for h in range(2) for pair in range(pairs)]


def dft_kernel(
    pairs, bins_hbm, mic_hbm, grid_hbm, signal_ref,
    out_ref, cos_ref, sin_ref, left_ref, right_ref,
    held, total, bins_ref, mic_ref, grid_ref, rows8, small_sem, sem,
):
    snaps, samples, mics = held.shape
    small = [
        pltpu.make_async_copy(source, target, small_sem.at[i])
        for i, (source, target) in enumerate([(bins_hbm, bins_ref), (mic_hbm, mic_ref), (grid_hbm, grid_ref)])
    ]

    def copy(s):
        return pltpu.make_async_copy(signal_ref.at[s], held.at[s], sem.at[s])

    for s in range(snaps):
        copy(s).start(priority=1)
    for c in small:
        c.start()
    for c in small:
        c.wait()
    index, core = lax.axis_index("near") * pairs + lax.axis_index("pair"), lax.axis_index("core")
    scale = bins_ref[index].astype(F32) * (RATE_OVER_SOUND / samples)
    order = mic_order(pairs, mics, core)
    distance_factors(scale, mic_ref, order, grid_ref, core * (grid_ref.shape[1] // 2), rows8, left_ref, right_ref)
    table = dft_table(bins_ref, samples)

    def transform(s, at, width):
        across = slice(at, at + width)
        total[s, :, across] = jnp.dot(table, held[s, :, across], preferred_element_type=F32)

    columns = min(COLUMNS, mics)
    points, lanes = cos_ref.shape
    step = min(STEP, lanes)
    row = snap = 0
    for snap_end, row_end in stages(snaps, points):
        for s in range(snap, snap_end):
            copy(s).wait()
        transforms = [(s, at, columns) for s in range(snap, snap_end) for at in range(0, mics, columns)]
        steerings = [(row, row_end, at, step) for at in range(0, lanes, step)]
        for take_transforms, take_steerings in interleaved(transforms, steerings):
            for args in take_transforms:
                transform(*args)
            for args in take_steerings:
                steer_block(*args, left_ref, right_ref, cos_ref, sin_ref)
        row, snap = row_end, snap_end
    for at in range(0, mics, columns):
        across = slice(at, at + columns)
        turned = jnp.transpose(total[:, :, across], (1, 0, 2))
        for f in range(F):
            out_ref[f, :, across] = jnp.concatenate([turned[f], turned[F + f]], 0).astype(BF16)


def project(nears, pairs, side, x_ref, cos_ref, sin_ref, real_lhs, swap_lhs, power):
    blocks, rows, mics = x_ref.shape
    half = rows // 2
    for pair in range(pairs):
        lanes = slice(pair * mics, (pair + 1) * mics)
        squares = jnp.zeros((half, mics), F32)
        for near in range(nears):
            block = x_ref[near * pairs + pair]
            real_lhs[near * rows : (near + 1) * rows, lanes] = block
            block = block.astype(F32)
            top, low = block[:half], block[half:]
            swap_lhs[near * rows : (near + 1) * rows, lanes] = jnp.concatenate([-low, top], 0).astype(BF16)
            squares = squares + (top * top + low * low)
        power[:, lanes] = jnp.broadcast_to(jnp.sum(squares, axis=0, keepdims=True), (8, mics))
    width = pairs * mics
    first = side * width
    form = (((1,), (1,)), ((), ()))
    step = min(COLUMNS, width)
    points = cos_ref.shape[0]
    y = 0.0
    diagonal = 0.0
    for at in range(0, width, step):
        here = slice(at, at + step)
        cos = cos_ref[:, first + at : first + at + step]
        sin = sin_ref[:, first + at : first + at + step]
        y = y + lax.dot_general(cos, real_lhs[:, here], form, preferred_element_type=F32)
        y = y + lax.dot_general(sin, swap_lhs[:, here], form, preferred_element_type=F32)
        cos = cos.astype(F32)
        sin = sin.astype(F32)
        weighted = (cos * cos + sin * sin) * power[0:1, here]
        for lane in range(0, step, LANES):
            diagonal = diagonal + weighted[:, lane : lane + LANES]
    return y, diagonal


def own_kernel(nears, pairs, x_ref, cos_ref, sin_ref, y_ref, diagonal_ref, real_lhs, swap_lhs, power):
    y_ref[...], diagonal_ref[...] = project(nears, pairs, 0, x_ref, cos_ref, sin_ref, real_lhs, swap_lhs, power)


def other_kernel(
    nears, pairs, x_ref, cos_ref, sin_ref, y_ref, diagonal_ref, out_ref, real_lhs, swap_lhs, power
):
    y, diagonal = project(nears, pairs, 1, x_ref, cos_ref, sin_ref, real_lhs, swap_lhs, power)
    y = y + y_ref[...]
    value = y * y
    if value.shape[1] % LANES:
        value = jnp.concatenate([value, jnp.zeros((value.shape[0], -value.shape[1] % LANES), F32)], 1)
    total = -(diagonal + diagonal_ref[...])
    for lane in range(0, value.shape[1], LANES):
        total = total + value[:, lane : lane + LANES]
    for block in range(out_ref.shape[1]):
        line = jnp.sum(total[block * LANES : (block + 1) * LANES].T, axis=0, keepdims=True)
        out_ref[:, block : block + 1, :] = jnp.broadcast_to(line[None], (out_ref.shape[0], 1, LANES))


def shards(nears, pairs, devices, signal, bins, mic_positions, grid_positions):
    snaps, samples, mics = signal.shape
    total_mics = mic_positions.shape[1]
    points = grid_positions.shape[1]
    half_points = points // 2
    vmem = pl.BlockSpec(memory_space=pltpu.VMEM)
    anywhere = pl.BlockSpec(memory_space=pl.ANY)

    def steer_shape(count):
        return [pltpu.VMEM((count, total_mics), BF16)] * 2

    def in_hbm(array):
        return pltpu.with_memory_space_constraint(array, pltpu.HBM)

    def in_vmem(array):
        return pltpu.with_memory_space_constraint(array, pltpu.VMEM)

    local, cos, sin = pl.pallas_call(
        functools.partial(dft_kernel, pairs),
        in_specs=[anywhere] * 4,
        out_specs=[vmem] * 3,
        out_shape=[
            jax.ShapeDtypeStruct((F, 2 * snaps, mics), BF16),
            *steer_shape(half_points),
        ],
        scratch_shapes=[
            pltpu.VMEM((half_points, LANES), BF16),
            pltpu.VMEM((DEPTH, total_mics), BF16),
            pltpu.VMEM((snaps, samples, mics), BF16),
            pltpu.VMEM((snaps, 2 * F, mics), F32),
            pltpu.SMEM(bins.shape, jnp.int32),
            pltpu.VMEM(mic_positions.shape, F32),
            pltpu.VMEM(grid_positions.shape, F32),
            pltpu.VMEM((8, total_mics), F32),
            pltpu.SemaphoreType.DMA((3,)),
            pltpu.SemaphoreType.DMA((snaps,)),
        ],
        compiler_params=pltpu.CompilerParams(vmem_limit_bytes=24 * 2**20),
        name="dft_and_steering",
    )(in_hbm(bins), in_hbm(mic_positions), in_hbm(grid_positions), in_hbm(signal))
    own = lax.all_to_all(local, ("near", "pair"), 0, 0, tiled=True)
    other = lax.ppermute(own, "core", [(0, 1), (1, 0)])
    wide = nears * 2 * snaps
    side_mics = total_mics // 2
    scratch = [
        pltpu.VMEM((wide, side_mics), BF16),
        pltpu.VMEM((wide, side_mics), BF16),
        pltpu.VMEM((8, side_mics), F32),
    ]
    steer = (in_vmem(cos), in_vmem(sin))
    cost = pl.CostEstimate(
        flops=4 * half_points * wide * side_mics, bytes_accessed=4 * half_points * side_mics, transcendentals=0
    )
    y, diagonal = pl.pallas_call(
        functools.partial(own_kernel, nears, pairs),
        in_specs=[vmem] * 3,
        out_specs=[vmem] * 2,
        out_shape=[pltpu.VMEM((half_points, wide), F32), pltpu.VMEM((half_points, LANES), F32)],
        scratch_shapes=scratch,
        compiler_params=pltpu.CompilerParams(vmem_limit_bytes=8 * 2**20),
        cost_estimate=cost,
        name="own_projection",
    )(own, *steer)
    mine = pl.pallas_call(
        functools.partial(other_kernel, nears, pairs),
        in_specs=[vmem] * 5,
        out_specs=vmem,
        out_shape=jax.ShapeDtypeStruct((devices, half_points // LANES, LANES), F32),
        scratch_shapes=scratch,
        compiler_params=pltpu.CompilerParams(vmem_limit_bytes=8 * 2**20),
        cost_estimate=cost,
        name="other_projection",
    )(other, *steer, in_vmem(y), in_vmem(diagonal))
    axes = ("wide", "near", "pair", "core")
    everyone = lax.all_to_all(mine, axes, 0, 0, tiled=True)
    summed = jnp.sum(everyone.reshape(-1, F, points), axis=0)
    all_snaps = snaps * lax.axis_size("wide") * nears
    return summed * (1.0 / (math.sqrt(all_snaps) * total_mics))


def solution(mesh):
    groups, inner = mesh.shape["grp"], mesh.shape["inner"]
    pairs = inner // 2
    nears = F // pairs
    fine = Mesh(mesh.devices.reshape(groups // nears, nears, pairs, 2), ("wide", "near", "pair", "core"))
    in_specs = (P(("wide", "near"), None, ("pair", "core")), P(), P(), P())
    step = functools.partial(shards, nears, pairs, groups * inner)
    return jax.shard_map(step, mesh=fine, in_specs=in_specs, out_specs=P(), check_vma=False)
```
